1024 devices in a mesh: wide: 16 (over x, core), tp: 64 (over z, y).
Axes of the slice: x: 8, y: 8, z: 8, core: 2. Of those that a mesh axis runs over, the one named last changes fastest.
Arguments:
- queries: bfloat16 [16, 64, 192, 1024], P('wide', 'tp')
- own_kv: bfloat16 [2, 16, 64, 192, 128], P(None, 'wide', 'tp'), may hold values from -6 to 6
- doc_kv: bfloat16 [2, 32, 128, 1024], P(None, 'wide', 'tp'), may hold values from -6 to 6
- doc_lengths: int32 [32], replicated, may hold values from 16 to 128, as said below
- doc_ids: int32 [128, 8], replicated, may hold values from 0 to 31, as said below
- d_out: bfloat16 [16, 64, 192, 1024], P('wide', 'tp'), may hold values from -6 to 6
Outputs:
- attended: bfloat16 [16, 64, 192, 1024], P('wide', 'tp')
- d_queries: bfloat16 [16, 64, 192, 1024], P('wide', 'tp')
- d_doc_kv: float32 [2, 32, 128, 1024], P(None, 'wide', 'tp')
The draws below stay inside these ranges and needn't reach their ends.
Inputs may be any that keep to these rules, and one draw needn't show every extreme that they name: `doc_ids`: each row names 8 documents whose owners, document // 2, are all different. `doc_lengths`: the longest document fills its whole block.
All inputs are finite; a program needn't handle non-finite values.
Results may differ from the reference program's by a relative error of at most 0.028.
Values may be sent and summed in bfloat16 or wider, within the bound.
No kernel may reach another device: no remote copies, remote signals or barrier semaphores. Data moves between devices by JAX's collectives and lax.ppermute only.
A program may use at most 32 MiB of HBM per device.

```python
import math
import jax
import jax.numpy as jnp
from jax import lax

HD = 128
KVH = 8
GROUP = 8
LEN = 192
DLEN = 128
DOC_DEV = 2
DOCS = 32
RSUB = 8
ROLLOUTS = 128
USES = 8
N_WIDE = 16
N_TP = 64


def draw_queries(key, part):
    key = jax.random.fold_in(key, 11)
    first_key = jax.random.fold_in(key, 0)
    base_draw = jax.random.normal(first_key, (N_WIDE, N_TP, LEN, GROUP * HD), jnp.float32)
    return jnp.clip(base_draw, -5.0, 5.0).astype(jnp.bfloat16)


def draw_doc_lengths(key, part):
    key = jax.random.fold_in(key, 37)
    first_key, second_key, third_key = jax.random.split(key, 3)
    lengths = jax.random.randint(first_key, (DOCS,), DLEN // 8, DLEN + 1)
    longest = jax.random.randint(second_key, (), 0, DOCS)
    shortest = (longest + 1 + jax.random.randint(third_key, (), 0, DOCS - 1)) % DOCS
    places = jnp.arange(DOCS)
    lengths = jnp.where(places == longest, DLEN, lengths)
    lengths = jnp.where(places == shortest, DLEN // 8, lengths)
    return lengths.astype(jnp.int32)


def move_front(order, wanted_owner):
    found_spot = jnp.argmax((order == wanted_owner).astype(jnp.int32))
    first_owner = order[0]
    return order.at[found_spot].set(first_owner).at[0].set(wanted_owner)


def draw_doc_ids(key, part):
    key = jax.random.fold_in(key, 23)
    first_key, second_key = jax.random.split(key)
    orders = jax.vmap(lambda single: jax.random.permutation(single, N_WIDE))(jax.random.split(first_key, ROLLOUTS))
    orders = orders.astype(jnp.int32)
    orders = orders.at[0].set(move_front(orders[0], N_WIDE - 1))
    orders = orders.at[1].set(move_front(orders[1], 0))
    owners = orders[:, :USES]
    within = jax.random.randint(second_key, (ROLLOUTS, USES), 0, DOC_DEV).astype(jnp.int32)
    within = within.at[0, 0].set(DOC_DEV - 1).at[1, 0].set(0)
    return (owners * DOC_DEV + within).astype(jnp.int32)


def levels(own_key, extent, cuts, least, largest):
    def one(axis_at, parts):
        heights = jax.random.uniform(jax.random.fold_in(jax.random.fold_in(own_key, 6), axis_at), (parts,), jnp.float32, least / len(cuts), largest / len(cuts))
        return jnp.repeat(jnp.exp(heights), extent[axis_at] // parts).reshape((-1,) + (1,) * (len(extent) - axis_at - 1))

    loudness = one(*cuts[0])
    for cut in cuts[1:]:
        loudness = loudness * one(*cut)
    return loudness


def noise(stream_key, dims, deviation, reach, pieces=(), kind=jnp.bfloat16):
    entries = deviation * jax.random.normal(stream_key, dims, jnp.float32)
    if pieces:
        entries = entries * levels(stream_key, dims, pieces, -0.22, 0.18)
    return jnp.clip(entries, -reach, reach).astype(kind)


def setup_inputs(seed: int = 0) -> dict:
    key_of = jax.random.split(jax.random.key(seed), 7)
    queries = draw_queries(jax.random.fold_in(key_of[6], 71), 0)
    own_kv = noise(key_of[1], (2, N_WIDE, N_TP, LEN, HD), 1.0, 6.0, ((1, 16), (2, 64)))
    doc_kv = noise(key_of[2], (2, DOCS, DLEN, KVH * HD), 1.0, 6.0, ((1, 16), (2, 64)))
    doc_lengths = draw_doc_lengths(jax.random.fold_in(key_of[6], 71), 0)
    doc_ids = draw_doc_ids(jax.random.fold_in(key_of[6], 71), 0)
    d_out = noise(key_of[5], (N_WIDE, N_TP, LEN, GROUP * HD), 1.0, 6.0, ((0, 16), (1, 64)))
    return {"queries": queries, "own_kv": own_kv, "doc_kv": doc_kv, "doc_lengths": doc_lengths, "doc_ids": doc_ids, "d_out": d_out}


def attend_head(query_rows, key_rows, value_rows, allowed, grad_rows):
    scale_factor = 1.0 / math.sqrt(query_rows.shape[1])
    scores = jnp.dot(query_rows, key_rows.T, preferred_element_type=jnp.float32) * scale_factor
    scores = jnp.where(allowed, scores, -1e+30)
    row_max = lax.optimization_barrier(jnp.max(scores, axis=1, keepdims=True))
    row_total = lax.optimization_barrier(jnp.sum(jnp.where(allowed, jnp.exp(scores - row_max), 0.0), axis=1, keepdims=True))
    weights = jnp.where(allowed, jnp.exp(scores - (row_max + jnp.log(row_total))), 0.0)
    weights_low = weights.astype(jnp.bfloat16)
    attended = jnp.dot(weights_low, value_rows, preferred_element_type=jnp.float32).astype(jnp.bfloat16)
    d_weights = jnp.dot(grad_rows, value_rows.T, preferred_element_type=jnp.float32)
    row_dot = lax.optimization_barrier(jnp.sum(grad_rows.astype(jnp.float32) * attended.astype(jnp.float32), axis=1, keepdims=True))
    d_scores = (weights * (d_weights - row_dot)).astype(jnp.bfloat16)
    d_query = (jnp.dot(d_scores, key_rows, preferred_element_type=jnp.float32) * scale_factor).astype(jnp.bfloat16)
    d_keys = jnp.dot(d_scores.T, query_rows, preferred_element_type=jnp.float32) * scale_factor
    d_values = jnp.dot(weights_low.T, grad_rows, preferred_element_type=jnp.float32)
    return (attended, d_query, d_keys, d_values)

def reference(queries, own_kv, doc_kv, doc_lengths, doc_ids, d_out):
    positions = jnp.arange(LEN)
    causal = positions[None, :] <= positions[:, None]
    doc_positions = jnp.arange(DLEN)

    def per_rollout(grad_total, rollout):
        group_index = rollout // RSUB
        sub_index = rollout % RSUB
        chosen = doc_ids[rollout]
        picked = doc_kv[:, chosen].reshape(2, USES * DLEN, KVH * HD)
        lengths = doc_lengths[chosen]
        doc_valid = (doc_positions[None, :] < lengths[:, None]).reshape(1, USES * DLEN)
        allowed = jnp.concatenate([jnp.broadcast_to(doc_valid, (LEN, USES * DLEN)), causal], axis=1)

        def per_kv_head(kv_head):
            slot_index = sub_index * KVH + kv_head
            query_block = queries[group_index, slot_index]
            grad_block = d_out[group_index, slot_index]
            own_rows = own_kv[:, group_index, slot_index]
            kv_start = (kv_head * HD).astype(jnp.int32)
            key_rows = jnp.concatenate([lax.dynamic_slice_in_dim(picked[0], kv_start, HD, 1), own_rows[0]], axis=0)
            value_rows = jnp.concatenate([lax.dynamic_slice_in_dim(picked[1], kv_start, HD, 1), own_rows[1]], axis=0)

            def per_head(head_slot):
                q_start = (head_slot * HD).astype(jnp.int32)
                query_rows = lax.dynamic_slice_in_dim(query_block, q_start, HD, 1)
                grad_rows = lax.dynamic_slice_in_dim(grad_block, q_start, HD, 1)
                attended, d_query, d_keys, d_values = attend_head(query_rows, key_rows, value_rows, allowed, grad_rows)
                return (attended, d_query, jnp.stack([d_keys[:USES * DLEN], d_values[:USES * DLEN]]))
            attended, d_query, head_grads = lax.map(per_head, jnp.arange(GROUP, dtype=jnp.int32))
            attended = attended.transpose(1, 0, 2).reshape(LEN, GROUP * HD)
            d_query = d_query.transpose(1, 0, 2).reshape(LEN, GROUP * HD)
            return (attended, d_query, lax.optimization_barrier(jnp.sum(head_grads, axis=0)))
        attended, d_query, doc_grads = lax.map(per_kv_head, jnp.arange(KVH, dtype=jnp.int32))
        doc_grads = doc_grads.reshape(KVH, 2, USES, DLEN, HD).transpose(1, 2, 3, 0, 4).reshape(2, USES, DLEN, KVH * HD)
        grad_total = grad_total.at[:, chosen].add(doc_grads)
        return (grad_total, (attended, d_query))
    start_grads = jnp.zeros((2, DOCS, DLEN, KVH * HD), jnp.float32)
    d_doc_kv, (attended, d_queries) = lax.scan(per_rollout, start_grads, jnp.arange(ROLLOUTS, dtype=jnp.int32))
    attended = attended.reshape(N_WIDE, RSUB * KVH, LEN, GROUP * HD)
    d_queries = d_queries.reshape(N_WIDE, RSUB * KVH, LEN, GROUP * HD)
    return (attended, d_queries, d_doc_kv)
```

```python
import functools
import math

import jax
import jax.numpy as jnp
from jax import lax
from jax.experimental import pallas as pl
from jax.experimental.pallas import tpu as pltpu
from jax.sharding import PartitionSpec as P

NT = (((1,), (1,)), ((), ()))
NN = (((1,), (0,)), ((), ()))
TN = (((0,), (0,)), ((), ()))
OUT_OF_REACH = -2e38


def dot(a, b, dims):
    return lax.dot_general(a, b, dims, preferred_element_type=jnp.float32)


def attention_kernel(heads, uses, q_ref, g_ref, own_ref, limit_ref, doc_ref, att_ref, dq_ref, dkv_ref, dk_sum, dv_sum):
    slots, head_dim = dk_sum.shape
    rows = q_ref.shape[0]
    scale = 1.0 / math.sqrt(head_dim)
    exponent = scale * math.log2(math.e)
    doc_k = doc_ref[:, 0].reshape(slots, head_dim)
    doc_v = doc_ref[:, 1].reshape(slots, head_dim)
    own_k, own_v = own_ref[0], own_ref[1]
    token = lax.broadcasted_iota(jnp.int32, (1, slots), 1) // uses
    doc_allowed = token < limit_ref[...]
    causal = lax.broadcasted_iota(jnp.int32, (rows, rows), 1) <= lax.broadcasted_iota(
        jnp.int32, (rows, rows), 0
    )
    for h in range(heads):
        cols = pl.ds(h * head_dim, head_dim)
        q, g = q_ref[:, cols], g_ref[:, cols]
        s_doc = jnp.where(doc_allowed, dot(q, doc_k, NT), OUT_OF_REACH)
        s_own = jnp.where(causal, dot(q, own_k, NT), OUT_OF_REACH)
        top = jnp.maximum(
            jnp.max(s_doc, axis=1, keepdims=True), jnp.max(s_own, axis=1, keepdims=True)
        )
        e_doc = jnp.exp2((s_doc - top) * exponent)
        e_own = jnp.exp2((s_own - top) * exponent)
        total = jnp.sum(e_doc, axis=1, keepdims=True) + jnp.sum(e_own, axis=1, keepdims=True)
        inverse = 1.0 / total
        w_doc, w_own = e_doc * inverse, e_own * inverse
        w_doc_low, w_own_low = w_doc.astype(jnp.bfloat16), w_own.astype(jnp.bfloat16)
        att = (dot(w_doc_low, doc_v, NN) + dot(w_own_low, own_v, NN)).astype(jnp.bfloat16)
        att_ref[:, cols] = att
        row_dot = jnp.sum(
            g.astype(jnp.float32) * att.astype(jnp.float32), axis=1, keepdims=True
        )
        ds_doc = (w_doc * (dot(g, doc_v, NT) - row_dot)).astype(jnp.bfloat16)
        ds_own = (w_own * (dot(g, own_v, NT) - row_dot)).astype(jnp.bfloat16)
        dq_ref[:, cols] = (
            (dot(ds_doc, doc_k, NN) + dot(ds_own, own_k, NN)) * scale
        ).astype(jnp.bfloat16)
        dk, dv = dot(ds_doc, q, TN), dot(w_doc_low, g, TN)
        if h:
            dk, dv = dk_sum[...] + dk, dv_sum[...] + dv
        if h < heads - 1:
            dk_sum[...] = dk
            dv_sum[...] = dv
        else:
            dkv_ref[:, 0] = (dk * scale).astype(jnp.bfloat16).reshape(doc_ref.shape[0], -1, head_dim)
            dkv_ref[:, 1] = dv.astype(jnp.bfloat16).reshape(doc_ref.shape[0], -1, head_dim)


def attention(q, g, own, limits, docs, uses):
    rows, width = q.shape
    head_dim = own.shape[2]
    heads = width // head_dim
    slots = limits.shape[1]
    vmem = pl.BlockSpec(memory_space=pltpu.VMEM)
    return pl.pallas_call(
        functools.partial(attention_kernel, heads, uses),
        out_shape=(
            jax.ShapeDtypeStruct(q.shape, jnp.bfloat16),
            jax.ShapeDtypeStruct(q.shape, jnp.bfloat16),
            jax.ShapeDtypeStruct(docs.shape, jnp.bfloat16),
        ),
        in_specs=[vmem] * 5,
        out_specs=(vmem,) * 3,
        scratch_shapes=[pltpu.VMEM((slots, head_dim), jnp.float32)] * 2,
        compiler_params=pltpu.CompilerParams(vmem_limit_bytes=48 * 1024 * 1024),
        cost_estimate=pl.CostEstimate(
            flops=12 * heads * rows * (slots + rows) * head_dim,
            bytes_accessed=4 * 2 * q.size + 2 * 2 * docs.size,
            transcendentals=heads * rows * (slots + rows),
        ),
    )(q, g, own, limits, docs)


def shards(queries, own_kv, doc_kv, doc_lengths, doc_ids, d_out):
    tp_width = lax.axis_size("tp")
    wide_width = lax.axis_size("wide")
    my_group = lax.axis_index("wide")
    head_dim = own_kv.shape[4]
    kv_heads = doc_kv.shape[3] // head_dim
    subs = tp_width // kv_heads
    my_sub = lax.axis_index("tp") // kv_heads
    docs_here, block_len = doc_kv.shape[1:3]
    uses = doc_ids.shape[1]
    slots = tp_width * block_len * uses

    slab = doc_kv.transpose(1, 0, 2, 3).reshape(-1, head_dim)
    every = lax.all_gather(slab, "wide", axis=0, tiled=False)
    every = every.reshape(wide_width, docs_here, 2, block_len, kv_heads, head_dim)

    by_sub = lax.dynamic_index_in_dim(
        doc_ids.reshape(wide_width, subs, uses), my_group, 0, keepdims=False
    )
    reads = (
        by_sub[:, :, None] == jnp.arange(wide_width * docs_here, dtype=jnp.int32)
    ).astype(jnp.bfloat16)
    reads = reads.reshape(subs, uses, wide_width, docs_here)
    chosen = lax.dynamic_index_in_dim(by_sub, my_sub, 0, keepdims=False)
    limits = jnp.tile(jnp.take(doc_lengths, chosen), slots // uses)[None]

    picked = jnp.einsum(
        "zuwd,wdkthl->zhktul", reads, every, preferred_element_type=jnp.float32
    ).astype(jnp.bfloat16)
    picked = picked.reshape(tp_width, 2, block_len * uses, head_dim)
    docs = lax.all_to_all(picked, "tp", 0, 0, tiled=True)

    attended, d_query, d_docs = attention(
        queries[0, 0], d_out[0, 0], own_kv[:, 0, 0], limits, docs, uses
    )

    back = lax.all_to_all(d_docs, "tp", 0, 0, tiled=True)
    back = back.reshape(subs, kv_heads, 2, block_len, uses, head_dim)
    by_doc = jnp.einsum(
        "zuwd,zhktul->wdkthl", reads, back, preferred_element_type=jnp.float32
    ).astype(jnp.bfloat16)
    by_doc = by_doc.reshape(wide_width, -1, head_dim)
    parts = lax.all_to_all(by_doc, "wide", 0, 0, tiled=True)
    d_doc = jnp.sum(parts.astype(jnp.float32), axis=0)
    d_doc = d_doc.reshape(docs_here, 2, block_len, kv_heads * head_dim).transpose(1, 0, 2, 3)
    return attended[None, None], d_query[None, None], d_doc


def solution(mesh):
    placed = (
        P("wide", "tp", None, None),
        P(None, "wide", "tp", None, None),
        P(None, "wide", "tp", None),
        P(),
        P(),
        P("wide", "tp", None, None),
    )
    return jax.shard_map(
        shards,
        mesh=mesh,
        in_specs=placed,
        out_specs=(
            P("wide", "tp", None, None),
            P("wide", "tp", None, None),
            P(None, "wide", "tp", None),
        ),
        check_vma=False,
    )
```

```python
import functools
import math

import jax
import jax.numpy as jnp
from jax import lax
from jax.experimental import pallas as pl
from jax.experimental.pallas import tpu as pltpu
from jax.sharding import PartitionSpec as P

NT = (((1,), (1,)), ((), ()))
NN = (((1,), (0,)), ((), ()))
TN = (((0,), (0,)), ((), ()))
OUT_OF_REACH = -2e38
STACK = 4


def dot(a, b, dims):
    return lax.dot_general(a, b, dims, preferred_element_type=jnp.float32)


def attention_kernel(heads, uses, q_ref, g_ref, own_ref, limit_ref, doc_ref, att_ref, dq_ref, dkv_ref, dk_sum, dv_sum):
    low = jnp.bfloat16
    sources, _, per_source, head_dim = doc_ref.shape
    slots = sources * per_source
    rows = q_ref.shape[0]
    scale = 1.0 / math.sqrt(head_dim)
    exponent = scale * math.log2(math.e)
    doc_k = doc_ref[:, 0].reshape(slots, head_dim)
    doc_v = doc_ref[:, 1].reshape(slots, head_dim)
    own_k, own_v = own_ref[0], own_ref[1]
    token = lax.broadcasted_iota(jnp.int32, (1, slots), 1) // uses
    doc_allowed = token < limit_ref[...]
    causal = lax.broadcasted_iota(jnp.int32, (rows, rows), 1) <= lax.broadcasted_iota(
        jnp.int32, (rows, rows), 0
    )
    causal = jnp.concatenate([causal.astype(jnp.int32)] * STACK, axis=0) > 0

    def stacked(ref, first):
        return jnp.concatenate(
            [ref[:, pl.ds((first + h) * head_dim, head_dim)] for h in range(STACK)], axis=0
        )

    def unstack(ref, first, value):
        for h in range(STACK):
            ref[:, pl.ds((first + h) * head_dim, head_dim)] = value[h * rows : (h + 1) * rows]

    for first in range(0, heads, STACK):
        q, g = stacked(q_ref, first), stacked(g_ref, first)
        s_doc = jnp.where(doc_allowed, dot(q, doc_k, NT), OUT_OF_REACH)
        s_own = jnp.where(causal, dot(q, own_k, NT), OUT_OF_REACH)
        top = jnp.maximum(
            jnp.max(s_doc, axis=1, keepdims=True), jnp.max(s_own, axis=1, keepdims=True)
        )
        e_doc = jnp.exp2((s_doc - top) * exponent)
        e_own = jnp.exp2((s_own - top) * exponent)
        total = jnp.sum(e_doc, axis=1, keepdims=True) + jnp.sum(e_own, axis=1, keepdims=True)
        inverse = 1.0 / total
        w_doc, w_own = e_doc * inverse, e_own * inverse
        w_doc_low, w_own_low = w_doc.astype(low), w_own.astype(low)
        att = (dot(w_doc_low, doc_v, NN) + dot(w_own_low, own_v, NN)).astype(low)
        row_dot = jnp.sum(
            g.astype(jnp.float32) * att.astype(jnp.float32), axis=1, keepdims=True
        )
        ds_doc = (w_doc * (dot(g, doc_v, NT) - row_dot)).astype(low)
        ds_own = (w_own * (dot(g, own_v, NT) - row_dot)).astype(low)
        dq = ((dot(ds_doc, doc_k, NN) + dot(ds_own, own_k, NN)) * scale).astype(low)
        unstack(att_ref, first, att)
        unstack(dq_ref, first, dq)
        dk, dv = dot(q.T, ds_doc, NN), dot(g.T, w_doc_low, NN)
        if first:
            dk, dv = dk_sum[...] + dk, dv_sum[...] + dv
        if first + STACK < heads:
            dk_sum[...] = dk
            dv_sum[...] = dv
        else:
            dkv_ref[:, 0] = (dk.T * scale).astype(low).reshape(sources, per_source, head_dim)
            dkv_ref[:, 1] = dv.T.astype(low).reshape(sources, per_source, head_dim)


def attention(q, g, own, limits, docs, uses):
    rows, width = q.shape
    head_dim = own.shape[2]
    heads = width // head_dim
    slots = limits.shape[1]
    vmem = pl.BlockSpec(memory_space=pltpu.VMEM)
    return pl.pallas_call(
        functools.partial(attention_kernel, heads, uses),
        out_shape=(
            jax.ShapeDtypeStruct(q.shape, jnp.bfloat16),
            jax.ShapeDtypeStruct(q.shape, jnp.bfloat16),
            jax.ShapeDtypeStruct(docs.shape, jnp.bfloat16),
        ),
        in_specs=[vmem] * 5,
        out_specs=(vmem,) * 3,
        scratch_shapes=[pltpu.VMEM((head_dim, slots), jnp.float32)] * 2,
        compiler_params=pltpu.CompilerParams(vmem_limit_bytes=48 * 1024 * 1024),
        cost_estimate=pl.CostEstimate(
            flops=12 * heads * rows * (slots + rows) * head_dim,
            bytes_accessed=4 * 2 * q.size + 2 * 2 * docs.size,
            transcendentals=heads * rows * (slots + rows),
        ),
    )(q, g, own, limits, docs)


def select_kernel(reads_ref, every_ref, out_ref, rows_ref):
    owners, per_owner, head_dim = every_ref.shape
    subs, kv_heads, _, per_piece, _ = out_ref.shape
    docs_here = reads_ref.shape[1] // owners
    block_len = per_owner // (2 * docs_here * kv_heads)
    uses = per_piece // block_len
    rows_ref[...] = every_ref[...].astype(jnp.float32).reshape(owners * per_owner, head_dim)
    for kind in range(2):
        found = []
        for token in range(block_len):
            columns = []
            for h in range(kv_heads):
                of_head = [
                    rows_ref[pl.ds(((kind * docs_here + doc) * block_len + token) * kv_heads + h, owners, stride=per_owner), :]
                    for doc in range(docs_here)
                ]
                columns.append(jnp.concatenate(of_head, axis=0))
            table = jnp.concatenate(columns, axis=1).astype(jnp.bfloat16)
            found.append(dot(reads_ref[...], table, NN))
        for h in range(kv_heads):
            piece = [
                part[:, h * head_dim : (h + 1) * head_dim].reshape(subs, uses, head_dim)
                for part in found
            ]
            out_ref[:, h, kind] = jnp.concatenate(piece, axis=1).astype(jnp.bfloat16)


def select(reads, every, subs, kv_heads, per_piece):
    owners, per_owner, head_dim = every.shape
    vmem = pl.BlockSpec(memory_space=pltpu.VMEM)
    return pl.pallas_call(
        select_kernel,
        out_shape=jax.ShapeDtypeStruct((subs, kv_heads, 2, per_piece, head_dim), jnp.bfloat16),
        in_specs=[vmem] * 2,
        out_specs=vmem,
        scratch_shapes=[pltpu.VMEM((owners * per_owner, head_dim), jnp.float32)],
        compiler_params=pltpu.CompilerParams(vmem_limit_bytes=16 * 1024 * 1024),
        cost_estimate=pl.CostEstimate(
            flops=2 * reads.size * per_owner * head_dim,
            bytes_accessed=6 * every.size,
            transcendentals=0,
        ),
    )(reads, every)


def shards(queries, own_kv, doc_kv, doc_lengths, doc_ids, d_out):
    tp_width = lax.axis_size("tp")
    wide_width = lax.axis_size("wide")
    my_group = lax.axis_index("wide")
    head_dim = own_kv.shape[4]
    kv_heads = doc_kv.shape[3] // head_dim
    subs = tp_width // kv_heads
    my_sub = lax.axis_index("tp") // kv_heads
    docs_here, block_len = doc_kv.shape[1:3]
    uses = doc_ids.shape[1]
    slots = tp_width * block_len * uses

    slab = doc_kv.reshape(1, -1, head_dim)
    every = lax.all_to_all(
        jnp.broadcast_to(slab, (wide_width,) + slab.shape[1:]), "wide", 0, 0, tiled=True
    )
    doc_ids, doc_lengths, every = lax.optimization_barrier((doc_ids, doc_lengths, every))

    by_sub = lax.dynamic_index_in_dim(
        doc_ids.reshape(wide_width, subs, uses), my_group, 0, keepdims=False
    )
    order = jnp.arange(wide_width * docs_here, dtype=jnp.int32)
    order = order.reshape(wide_width, docs_here).T.reshape(-1)
    reads = (by_sub[:, :, None] == order).astype(jnp.bfloat16).reshape(subs * uses, -1)
    chosen = lax.dynamic_index_in_dim(by_sub, my_sub, 0, keepdims=False)
    lengths = jnp.sum(
        jnp.where(chosen[:, None] == jnp.arange(doc_lengths.shape[0], dtype=jnp.int32), doc_lengths, 0), axis=1
    )
    limits = jnp.tile(lengths, slots // uses)[None]

    picked = select(reads, every, subs, kv_heads, block_len * uses)
    picked = picked.reshape(tp_width, 2, block_len * uses, head_dim)
    picked, limits = lax.optimization_barrier((picked, limits))
    docs = lax.all_to_all(picked, "tp", 0, 0, tiled=True)

    attended, d_query, d_docs = attention(
        queries[0, 0], d_out[0, 0], own_kv[:, 0, 0], limits, docs, uses
    )

    back = lax.all_to_all(d_docs, "tp", 0, 0, tiled=True)
    back = back.reshape(subs, kv_heads, 2, block_len, uses, head_dim)
    by_doc = jnp.einsum(
        "zudw,zhktul->wkdthl",
        reads.reshape(subs, uses, docs_here, wide_width),
        back,
        preferred_element_type=jnp.float32,
    ).astype(jnp.bfloat16)
    by_doc = by_doc.reshape(wide_width, -1, head_dim)
    parts = lax.all_to_all(by_doc, "wide", 0, 0, tiled=True)
    d_doc = jnp.sum(parts.astype(jnp.float32), axis=0)
    d_doc = d_doc.reshape(2, docs_here, block_len, kv_heads * head_dim)
    return attended[None, None], d_query[None, None], d_doc


def solution(mesh):
    placed = (
        P("wide", "tp", None, None),
        P(None, "wide", "tp", None, None),
        P(None, "wide", "tp", None),
        P(),
        P(),
        P("wide", "tp", None, None),
    )
    return jax.shard_map(
        shards,
        mesh=mesh,
        in_specs=placed,
        out_specs=(
            P("wide", "tp", None, None),
            P("wide", "tp", None, None),
            P(None, "wide", "tp", None),
        ),
        check_vma=False,
    )
```

```python
import functools
import math

import jax
import jax.numpy as jnp
from jax import lax
from jax.experimental import pallas as pl
from jax.experimental.pallas import tpu as pltpu
from jax.sharding import PartitionSpec as P

NT = (((1,), (1,)), ((), ()))
NN = (((1,), (0,)), ((), ()))
TN = (((0,), (0,)), ((), ()))
OUT_OF_REACH = -2e38
STACK = 4


def dot(a, b, dims):
    return lax.dot_general(a, b, dims, preferred_element_type=jnp.float32)


def attention_kernel(heads, uses, q_ref, g_ref, own_ref, limit_ref, doc_ref, att_ref, dq_ref, dkv_ref, dk_sum, dv_sum):
    low = jnp.bfloat16
    sources, _, per_source, head_dim = doc_ref.shape
    slots = sources * per_source
    rows = q_ref.shape[0]
    scale = 1.0 / math.sqrt(head_dim)
    exponent = scale * math.log2(math.e)
    doc_k = doc_ref[:, 0].reshape(slots, head_dim)
    doc_v = doc_ref[:, 1].reshape(slots, head_dim)
    own_k, own_v = own_ref[0], own_ref[1]
    token = lax.broadcasted_iota(jnp.int32, (1, slots), 1) // uses
    doc_allowed = token < limit_ref[...]
    causal = lax.broadcasted_iota(jnp.int32, (rows, rows), 1) <= lax.broadcasted_iota(
        jnp.int32, (rows, rows), 0
    )
    causal = jnp.concatenate([causal.astype(jnp.int32)] * STACK, axis=0) > 0

    def stacked(ref, first):
        return jnp.concatenate(
            [ref[:, pl.ds((first + h) * head_dim, head_dim)] for h in range(STACK)], axis=0
        )

    def unstack(ref, first, value):
        for h in range(STACK):
            ref[:, pl.ds((first + h) * head_dim, head_dim)] = value[h * rows : (h + 1) * rows]

    for first in range(0, heads, STACK):
        q, g = stacked(q_ref, first), stacked(g_ref, first)
        s_doc = jnp.where(doc_allowed, dot(q, doc_k, NT), OUT_OF_REACH)
        s_own = jnp.where(causal, dot(q, own_k, NT), OUT_OF_REACH)
        top = jnp.maximum(
            jnp.max(s_doc, axis=1, keepdims=True), jnp.max(s_own, axis=1, keepdims=True)
        )
        e_doc = jnp.exp2((s_doc - top) * exponent)
        e_own = jnp.exp2((s_own - top) * exponent)
        total = jnp.sum(e_doc, axis=1, keepdims=True) + jnp.sum(e_own, axis=1, keepdims=True)
        inverse = 1.0 / total
        w_doc, w_own = e_doc * inverse, e_own * inverse
        w_doc_low, w_own_low = w_doc.astype(low), w_own.astype(low)
        att = (dot(w_doc_low, doc_v, NN) + dot(w_own_low, own_v, NN)).astype(low)
        row_dot = jnp.sum(
            g.astype(jnp.float32) * att.astype(jnp.float32), axis=1, keepdims=True
        )
        ds_doc = (w_doc * (dot(g, doc_v, NT) - row_dot)).astype(low)
        ds_own = (w_own * (dot(g, own_v, NT) - row_dot)).astype(low)
        dq = ((dot(ds_doc, doc_k, NN) + dot(ds_own, own_k, NN)) * scale).astype(low)
        unstack(att_ref, first, att)
        unstack(dq_ref, first, dq)
        dk, dv = dot(q.T, ds_doc, NN), dot(g.T, w_doc_low, NN)
        if first:
            dk, dv = dk_sum[...] + dk, dv_sum[...] + dv
        if first + STACK < heads:
            dk_sum[...] = dk
            dv_sum[...] = dv
        else:
            dkv_ref[:, 0] = (dk.T * scale).astype(low).reshape(sources, per_source, head_dim)
            dkv_ref[:, 1] = dv.T.astype(low).reshape(sources, per_source, head_dim)


def attention(q, g, own, limits, docs, uses):
    rows, width = q.shape
    head_dim = own.shape[2]
    heads = width // head_dim
    slots = limits.shape[1]
    vmem = pl.BlockSpec(memory_space=pltpu.VMEM)
    return pl.pallas_call(
        functools.partial(attention_kernel, heads, uses),
        out_shape=(
            jax.ShapeDtypeStruct(q.shape, jnp.bfloat16),
            jax.ShapeDtypeStruct(q.shape, jnp.bfloat16),
            jax.ShapeDtypeStruct(docs.shape, jnp.bfloat16),
        ),
        in_specs=[vmem] * 5,
        out_specs=(vmem,) * 3,
        scratch_shapes=[pltpu.VMEM((head_dim, slots), jnp.float32)] * 2,
        compiler_params=pltpu.CompilerParams(vmem_limit_bytes=48 * 1024 * 1024),
        cost_estimate=pl.CostEstimate(
            flops=12 * heads * rows * (slots + rows) * head_dim,
            bytes_accessed=4 * 2 * q.size + 2 * 2 * docs.size,
            transcendentals=heads * rows * (slots + rows),
        ),
    )(q, g, own, limits, docs)


def row_of(kind, doc, token, head, docs_here, block_len):
    return ((head * 2 + kind) * docs_here + doc) * block_len + token


def slab_kernel(doc_ref, out_ref):
    copies, per_owner, head_dim = out_ref.shape
    lines = doc_ref[...].reshape(-1, doc_ref.shape[3])
    heads = lines.shape[1] // head_dim
    slab = jnp.concatenate(
        [lines[:, h * head_dim : (h + 1) * head_dim] for h in range(heads)], axis=0
    )
    for i in range(copies):
        out_ref[i] = slab


def total_kernel(parts_ref, out_ref):
    owners, per_owner, head_dim = parts_ref.shape
    total = parts_ref[0].astype(jnp.float32)
    for i in range(1, owners):
        total = total + parts_ref[i].astype(jnp.float32)
    heads = out_ref.shape[3] // head_dim
    lines = per_owner // heads
    whole = jnp.concatenate(
        [total[h * lines : (h + 1) * lines] for h in range(heads)], axis=1
    )
    out_ref[...] = whole.reshape(out_ref.shape)


def select_kernel(ids_ref, lengths_ref, every_ref, out_ref, reads_ref, limit_ref, rows_ref):
    owners, per_owner, head_dim = every_ref.shape
    subs, kv_heads, _, per_piece, _ = out_ref.shape
    uses, rollouts = ids_ref.shape
    docs = lengths_ref.shape[1]
    docs_here = docs // owners
    block_len = per_piece // uses
    group = lax.axis_index("wide")
    my_sub = lax.axis_index("tp") // kv_heads

    ids = ids_ref[...].astype(jnp.float32)
    place = lax.broadcasted_iota(jnp.int32, (uses, rollouts), 1)

    def documents(sub):
        mine = place == group * subs + sub
        return jnp.sum(jnp.where(mine, ids, 0.0), axis=1, keepdims=True).astype(jnp.int32)

    column = lax.broadcasted_iota(jnp.int32, (uses, docs), 1)
    named = column % owners * docs_here + column // owners
    reads = jnp.concatenate(
        [(documents(sub) == named).astype(jnp.float32) for sub in range(subs)], axis=0
    ).astype(jnp.bfloat16)
    reads_ref[...] = reads

    lengths = lengths_ref[...].astype(jnp.float32)
    my_lengths = jnp.sum(
        jnp.where(documents(my_sub) == column, lengths, 0.0), axis=1, keepdims=True
    )
    wide_row = (uses, 128)
    use = lax.broadcasted_iota(jnp.int32, wide_row, 0)
    lane = lax.broadcasted_iota(jnp.int32, wide_row, 1)
    limits = jnp.sum(jnp.where(lane % uses == use, my_lengths, 0.0), axis=0, keepdims=True)
    limits = limits.astype(jnp.int32)
    limit_ref[...] = jnp.concatenate([limits] * (limit_ref.shape[1] // 128), axis=1)

    rows_ref[...] = every_ref[...].astype(jnp.float32).reshape(owners * per_owner, head_dim)
    for kind in range(2):
        found = []
        for token in range(block_len):
            columns = []
            for h in range(kv_heads):
                of_head = [
                    rows_ref[pl.ds(row_of(kind, doc, token, h, docs_here, block_len), owners, stride=per_owner), :]
                    for doc in range(docs_here)
                ]
                columns.append(jnp.concatenate(of_head, axis=0))
            table = jnp.concatenate(columns, axis=1).astype(jnp.bfloat16)
            found.append(dot(reads, table, NN))
        for h in range(kv_heads):
            piece = [
                part[:, h * head_dim : (h + 1) * head_dim].reshape(subs, uses, head_dim)
                for part in found
            ]
            out_ref[:, h, kind] = jnp.concatenate(piece, axis=1).astype(jnp.bfloat16)


def combine_kernel(reads_ref, back_ref, out_ref, rows_ref):
    owners, per_owner, head_dim = out_ref.shape
    subs, kv_heads, _, per_piece, _ = back_ref.shape
    docs_here = reads_ref.shape[1] // owners
    uses = reads_ref.shape[0] // subs
    block_len = per_piece // uses
    reads = reads_ref[...]
    for kind in range(2):
        pieces = [back_ref[:, h, kind].astype(jnp.float32) for h in range(kv_heads)]
        for token in range(block_len):
            table = jnp.concatenate(
                [
                    piece[:, token * uses : (token + 1) * uses].reshape(subs * uses, head_dim)
                    for piece in pieces
                ],
                axis=1,
            ).astype(jnp.bfloat16)
            sums = dot(reads, table, TN)
            for h in range(kv_heads):
                for doc in range(docs_here):
                    row = row_of(kind, doc, token, h, docs_here, block_len)
                    rows_ref[pl.ds(row, owners, stride=per_owner), :] = sums[
                        doc * owners : (doc + 1) * owners, h * head_dim : (h + 1) * head_dim
                    ]
    out_ref[...] = rows_ref[...].astype(jnp.bfloat16).reshape(out_ref.shape)


def local(kernel, out, *args, scratch=(), flops=0):
    vmem = pl.BlockSpec(memory_space=pltpu.VMEM)
    many = isinstance(out, tuple)
    size = sum(x.size * x.dtype.itemsize for x in args)
    return pl.pallas_call(
        kernel,
        out_shape=out,
        in_specs=[vmem] * len(args),
        out_specs=(vmem,) * len(out) if many else vmem,
        scratch_shapes=list(scratch),
        compiler_params=pltpu.CompilerParams(vmem_limit_bytes=16 * 1024 * 1024),
        cost_estimate=pl.CostEstimate(flops=flops, bytes_accessed=2 * size, transcendentals=0),
    )(*args)


def shards(queries, own_kv, doc_kv, doc_lengths, doc_ids, d_out):
    tp_width = lax.axis_size("tp")
    wide_width = lax.axis_size("wide")
    head_dim = own_kv.shape[4]
    kv_heads = doc_kv.shape[3] // head_dim
    subs = tp_width // kv_heads
    docs_here, block_len = doc_kv.shape[1:3]
    uses = doc_ids.shape[1]
    slots = tp_width * block_len * uses
    low = jnp.bfloat16
    per_owner = 2 * docs_here * block_len * kv_heads
    per_piece = block_len * uses

    slabs = jax.ShapeDtypeStruct((wide_width, per_owner, head_dim), low)
    pieces = jax.ShapeDtypeStruct((subs, kv_heads, 2, per_piece, head_dim), low)
    reads = jax.ShapeDtypeStruct((subs * uses, wide_width * docs_here), low)
    limits = jax.ShapeDtypeStruct((1, slots), jnp.int32)
    rows = pltpu.VMEM((wide_width * per_owner, head_dim), jnp.float32)
    flops = 2 * subs * uses * wide_width * docs_here * per_owner // docs_here * head_dim

    every = lax.all_to_all(local(slab_kernel, slabs, doc_kv), "wide", 0, 0, tiled=True)
    picked, reads, limits = local(
        select_kernel, (pieces, reads, limits), doc_ids.T, doc_lengths[None], every, scratch=(rows,), flops=flops
    )
    docs = lax.all_to_all(
        picked.reshape(tp_width, 2, per_piece, head_dim), "tp", 0, 0, tiled=True
    )

    attended, d_query, d_docs = attention(
        queries[0, 0], d_out[0, 0], own_kv[:, 0, 0], limits, docs, uses
    )

    back = lax.all_to_all(d_docs, "tp", 0, 0, tiled=True).reshape(pieces.shape)
    by_doc = local(combine_kernel, slabs, reads, back, scratch=(rows,), flops=flops)
    parts = lax.all_to_all(by_doc, "wide", 0, 0, tiled=True)
    d_doc = local(total_kernel, jax.ShapeDtypeStruct(doc_kv.shape, jnp.float32), parts)
    return attended[None, None], d_query[None, None], d_doc


def solution(mesh):
    placed = (
        P("wide", "tp", None, None),
        P(None, "wide", "tp", None, None),
        P(None, "wide", "tp", None),
        P(),
        P(),
        P("wide", "tp", None, None),
    )
    return jax.shard_map(
        shards,
        mesh=mesh,
        in_specs=placed,
        out_specs=(
            P("wide", "tp", None, None),
            P("wide", "tp", None, None),
            P(None, "wide", "tp", None),
        ),
        check_vma=False,
    )
```

```python
import functools
import math

import jax
import jax.numpy as jnp
from jax import lax
from jax.experimental import pallas as pl
from jax.experimental.pallas import tpu as pltpu
from jax.sharding import PartitionSpec as P

NT = (((1,), (1,)), ((), ()))
NN = (((1,), (0,)), ((), ()))
TN = (((0,), (0,)), ((), ()))
OUT_OF_REACH = -2e38
STACK = 4
VMEM_BYTES = 48 * 1024 * 1024


def dot(a, b, dims):
    return lax.dot_general(a, b, dims, preferred_element_type=jnp.float32)


def documents(ids_ref, subs, sub):
    uses, rollouts = ids_ref.shape
    place = lax.broadcasted_iota(jnp.int32, (uses, rollouts), 1)
    mine = place == lax.axis_index("wide") * subs + sub
    ids = jnp.where(mine, ids_ref[...].astype(jnp.float32), 0.0)
    return jnp.sum(ids, axis=1, keepdims=True).astype(jnp.int32)


def length_row(subs, kv_heads, slots, ids_ref, lengths_ref):
    mine = documents(ids_ref, subs, lax.axis_index("tp") // kv_heads)
    uses, docs = ids_ref.shape[0], lengths_ref.shape[1]
    column = lax.broadcasted_iota(jnp.int32, (uses, docs), 1)
    lengths = jnp.where(mine == column, lengths_ref[...].astype(jnp.float32), 0.0)
    lengths = jnp.sum(lengths, axis=1, keepdims=True)
    use = lax.broadcasted_iota(jnp.int32, (uses, 128), 0)
    lane = lax.broadcasted_iota(jnp.int32, (uses, 128), 1)
    row = jnp.sum(jnp.where(lane % uses == use, lengths, 0.0), axis=0, keepdims=True)
    return jnp.concatenate([row.astype(jnp.int32)] * (slots // 128), axis=1)


class Rollout:
    def __init__(self, uses, q_ref, g_ref, own_ref, doc_ref, limits):
        self.q_ref, self.g_ref = q_ref, g_ref
        sources, _, per_source, self.head_dim = doc_ref.shape
        self.rows = q_ref.shape[0]
        self.heads = q_ref.shape[1] // self.head_dim
        slots = sources * per_source
        self.scale = 1.0 / math.sqrt(self.head_dim)
        self.doc_k = doc_ref[:, 0].reshape(slots, self.head_dim)
        self.doc_v = doc_ref[:, 1].reshape(slots, self.head_dim)
        self.own_k, self.own_v = own_ref[0], own_ref[1]
        token = lax.broadcasted_iota(jnp.int32, (1, slots), 1) // uses
        self.doc_allowed = token < limits
        square = (self.rows, self.rows)
        causal = lax.broadcasted_iota(jnp.int32, square, 1) <= lax.broadcasted_iota(
            jnp.int32, square, 0
        )
        self.causal = jnp.concatenate([causal.astype(jnp.int32)] * STACK, axis=0) > 0

    def stacked(self, ref, first):
        return jnp.concatenate(
            [
                ref[:, pl.ds((first + h) * self.head_dim, self.head_dim)]
                for h in range(STACK)
            ],
            axis=0,
        )

    def unstack(self, ref, first, value):
        for h in range(STACK):
            ref[:, pl.ds((first + h) * self.head_dim, self.head_dim)] = value[
                h * self.rows : (h + 1) * self.rows
            ]

    def heads_from(self, first):
        low = jnp.bfloat16
        exponent = self.scale * math.log2(math.e)
        q, g = self.stacked(self.q_ref, first), self.stacked(self.g_ref, first)
        s_doc = jnp.where(self.doc_allowed, dot(q, self.doc_k, NT), OUT_OF_REACH)
        s_own = jnp.where(self.causal, dot(q, self.own_k, NT), OUT_OF_REACH)
        top = jnp.maximum(
            jnp.max(s_doc, axis=1, keepdims=True), jnp.max(s_own, axis=1, keepdims=True)
        )
        e_doc = jnp.exp2((s_doc - top) * exponent)
        e_own = jnp.exp2((s_own - top) * exponent)
        total = jnp.sum(e_doc, axis=1, keepdims=True) + jnp.sum(e_own, axis=1, keepdims=True)
        inverse = 1.0 / total
        w_doc, w_own = e_doc * inverse, e_own * inverse
        w_doc_low, w_own_low = w_doc.astype(low), w_own.astype(low)
        att = (dot(w_doc_low, self.doc_v, NN) + dot(w_own_low, self.own_v, NN)).astype(low)
        row_dot = jnp.sum(
            g.astype(jnp.float32) * att.astype(jnp.float32), axis=1, keepdims=True
        )
        ds_doc = (w_doc * (dot(g, self.doc_v, NT) - row_dot)).astype(low)

        def ds_own():
            return (w_own * (dot(g, self.own_v, NT) - row_dot)).astype(low)

        return q, g, w_doc_low, att, ds_doc, ds_own


def document_kernel(
    subs, kv_heads, q_ref, g_ref, own_ref, ids_ref, lengths_ref, doc_ref, dkv_ref, limit_ref, dk_sum, dv_sum
):
    low = jnp.bfloat16
    sources, _, per_source, head_dim = doc_ref.shape
    limits = length_row(subs, kv_heads, sources * per_source, ids_ref, lengths_ref)
    limit_ref[...] = limits
    rollout = Rollout(ids_ref.shape[0], q_ref, g_ref, own_ref, doc_ref, limits)
    for first in range(0, rollout.heads, STACK):
        q, g, w_doc, _, ds_doc, _ = rollout.heads_from(first)
        dk, dv = dot(q.T, ds_doc, NN), dot(g.T, w_doc, NN)
        if first:
            dk, dv = dk_sum[...] + dk, dv_sum[...] + dv
        if first + STACK < rollout.heads:
            dk_sum[...] = dk
            dv_sum[...] = dv
        else:
            dk = dk.T * rollout.scale
            dkv_ref[:, 0] = dk.astype(low).reshape(sources, per_source, head_dim)
            dkv_ref[:, 1] = dv.T.astype(low).reshape(sources, per_source, head_dim)


def query_kernel(uses, q_ref, g_ref, own_ref, limit_ref, doc_ref, att_ref, dq_ref, ready_ref):
    ready_ref[...] = limit_ref[...]
    rollout = Rollout(uses, q_ref, g_ref, own_ref, doc_ref, limit_ref[...])
    for first in range(0, rollout.heads, STACK):
        _, _, _, att, ds_doc, ds_own = rollout.heads_from(first)
        dq = dot(ds_doc, rollout.doc_k, NN) + dot(ds_own(), rollout.own_k, NN)
        rollout.unstack(att_ref, first, att)
        rollout.unstack(dq_ref, first, (dq * rollout.scale).astype(jnp.bfloat16))


def attention(q, g, own, ids, lengths, docs, subs, kv_heads):
    rows, width = q.shape
    head_dim = own.shape[2]
    slots = docs.size // (2 * head_dim)
    uses = ids.shape[0]
    vmem = pl.BlockSpec(memory_space=pltpu.VMEM)
    pairs = width // head_dim * rows * (slots + rows)

    def call(kernel, out, *args, scratch=()):
        return pl.pallas_call(
            kernel,
            out_shape=out,
            in_specs=[vmem] * len(args),
            out_specs=(vmem,) * len(out),
            scratch_shapes=list(scratch),
            compiler_params=pltpu.CompilerParams(vmem_limit_bytes=VMEM_BYTES),
            cost_estimate=pl.CostEstimate(
                flops=10 * pairs * head_dim,
                bytes_accessed=2 * (2 * q.size + 2 * docs.size),
                transcendentals=pairs,
            ),
        )(*args)

    d_docs, limits = call(
        functools.partial(document_kernel, subs, kv_heads),
        (
            jax.ShapeDtypeStruct(docs.shape, jnp.bfloat16),
            jax.ShapeDtypeStruct((1, slots), jnp.int32),
        ),
        q, g, own, ids, lengths, docs,
        scratch=[pltpu.VMEM((head_dim, slots), jnp.float32)] * 2,
    )
    attended, d_query, ready = call(
        functools.partial(query_kernel, uses),
        (jax.ShapeDtypeStruct(q.shape, jnp.bfloat16),) * 2
        + (jax.ShapeDtypeStruct(limits.shape, limits.dtype),),
        q, g, own, limits, docs,
    )
    return attended, d_query, ready, d_docs


def row_of(kind, doc, token, head, docs_here, block_len):
    return ((head * 2 + kind) * docs_here + doc) * block_len + token


def slab_kernel(doc_ref, out_ref):
    copies, per_owner, head_dim = out_ref.shape
    lines = doc_ref[...].reshape(-1, doc_ref.shape[3])
    heads = lines.shape[1] // head_dim
    slab = jnp.concatenate(
        [lines[:, h * head_dim : (h + 1) * head_dim] for h in range(heads)], axis=0
    )
    for i in range(copies):
        out_ref[i] = slab


def total_kernel(parts_ref, out_ref):
    owners, per_owner, head_dim = parts_ref.shape
    total = parts_ref[0].astype(jnp.float32)
    for i in range(1, owners):
        total = total + parts_ref[i].astype(jnp.float32)
    heads = out_ref.shape[3] // head_dim
    lines = per_owner // heads
    whole = jnp.concatenate(
        [total[h * lines : (h + 1) * lines] for h in range(heads)], axis=1
    )
    out_ref[...] = whole.reshape(out_ref.shape)


def select_kernel(ids_ref, every_ref, out_ref, reads_ref, rows_ref):
    owners, per_owner, head_dim = every_ref.shape
    subs, kv_heads, _, per_piece, _ = out_ref.shape
    uses = ids_ref.shape[0]
    docs = reads_ref.shape[1]
    docs_here = docs // owners
    block_len = per_piece // uses
    column = lax.broadcasted_iota(jnp.int32, (uses, docs), 1)
    named = column % owners * docs_here + column // owners
    reads = jnp.concatenate(
        [
            (documents(ids_ref, subs, sub) == named).astype(jnp.float32)
            for sub in range(subs)
        ],
        axis=0,
    ).astype(jnp.bfloat16)
    reads_ref[...] = reads
    rows_ref[...] = every_ref[...].astype(jnp.float32).reshape(owners * per_owner, head_dim)
    for kind in range(2):
        found = []
        for token in range(block_len):
            columns = []
            for h in range(kv_heads):
                of_head = [
                    rows_ref[pl.ds(row_of(kind, doc, token, h, docs_here, block_len), owners, stride=per_owner), :]
                    for doc in range(docs_here)
                ]
                columns.append(jnp.concatenate(of_head, axis=0))
            table = jnp.concatenate(columns, axis=1).astype(jnp.bfloat16)
            found.append(dot(reads, table, NN))
        for h in range(kv_heads):
            piece = [
                part[:, h * head_dim : (h + 1) * head_dim].reshape(subs, uses, head_dim)
                for part in found
            ]
            out_ref[:, h, kind] = jnp.concatenate(piece, axis=1).astype(jnp.bfloat16)


def combine_kernel(ready_ref, reads_ref, back_ref, out_ref, rows_ref):
    owners, per_owner, head_dim = out_ref.shape
    subs, kv_heads, _, per_piece, _ = back_ref.shape
    docs_here = reads_ref.shape[1] // owners
    uses = reads_ref.shape[0] // subs
    block_len = per_piece // uses
    reads = reads_ref[...]
    for kind in range(2):
        pieces = [back_ref[:, h, kind].astype(jnp.float32) for h in range(kv_heads)]
        for token in range(block_len):
            table = jnp.concatenate(
                [
                    piece[:, token * uses : (token + 1) * uses].reshape(subs * uses, head_dim)
                    for piece in pieces
                ],
                axis=1,
            ).astype(jnp.bfloat16)
            sums = dot(reads, table, TN)
            for h in range(kv_heads):
                for doc in range(docs_here):
                    row = row_of(kind, doc, token, h, docs_here, block_len)
                    rows_ref[pl.ds(row, owners, stride=per_owner), :] = sums[
                        doc * owners : (doc + 1) * owners, h * head_dim : (h + 1) * head_dim
                    ]
    out_ref[...] = rows_ref[...].astype(jnp.bfloat16).reshape(out_ref.shape)


def local(kernel, out, *args, scratch=(), flops=0):
    vmem = pl.BlockSpec(memory_space=pltpu.VMEM)
    many = isinstance(out, tuple)
    size = sum(x.size * x.dtype.itemsize for x in args)
    return pl.pallas_call(
        kernel,
        out_shape=out,
        in_specs=[vmem] * len(args),
        out_specs=(vmem,) * len(out) if many else vmem,
        scratch_shapes=list(scratch),
        compiler_params=pltpu.CompilerParams(vmem_limit_bytes=16 * 1024 * 1024),
        cost_estimate=pl.CostEstimate(flops=flops, bytes_accessed=2 * size, transcendentals=0),
    )(*args)


def shards(queries, own_kv, doc_kv, doc_lengths, doc_ids, d_out):
    tp_width = lax.axis_size("tp")
    wide_width = lax.axis_size("wide")
    head_dim = own_kv.shape[4]
    kv_heads = doc_kv.shape[3] // head_dim
    subs = tp_width // kv_heads
    docs_here, block_len = doc_kv.shape[1:3]
    uses = doc_ids.shape[1]
    low = jnp.bfloat16
    per_owner = 2 * docs_here * block_len * kv_heads
    per_piece = block_len * uses

    slabs = jax.ShapeDtypeStruct((wide_width, per_owner, head_dim), low)
    pieces = jax.ShapeDtypeStruct((subs, kv_heads, 2, per_piece, head_dim), low)
    reads = jax.ShapeDtypeStruct((subs * uses, wide_width * docs_here), low)
    ids = doc_ids.T
    rows = pltpu.VMEM((wide_width * per_owner, head_dim), jnp.float32)
    flops = 2 * subs * uses * wide_width * docs_here * per_owner // docs_here * head_dim

    every = lax.all_to_all(local(slab_kernel, slabs, doc_kv), "wide", 0, 0, tiled=True)
    picked, reads = local(
        select_kernel, (pieces, reads), ids, every, scratch=(rows,), flops=flops
    )
    docs = lax.all_to_all(
        picked.reshape(tp_width, 2, per_piece, head_dim), "tp", 0, 0, tiled=True
    )

    attended, d_query, ready, d_docs = attention(
        queries[0, 0], d_out[0, 0], own_kv[:, 0, 0], ids, doc_lengths[None], docs, subs, kv_heads
    )

    back = lax.all_to_all(d_docs, "tp", 0, 0, tiled=True).reshape(pieces.shape)
    by_doc = local(combine_kernel, slabs, ready, reads, back, scratch=(rows,), flops=flops)
    parts = lax.all_to_all(by_doc, "wide", 0, 0, tiled=True)
    d_doc = local(total_kernel, jax.ShapeDtypeStruct(doc_kv.shape, jnp.float32), parts)
    return attended[None, None], d_query[None, None], d_doc


def solution(mesh):
    placed = (
        P("wide", "tp", None, None),
        P(None, "wide", "tp", None, None),
        P(None, "wide", "tp", None),
        P(),
        P(),
        P("wide", "tp", None, None),
    )
    return jax.shard_map(
        shards,
        mesh=mesh,
        in_specs=placed,
        out_specs=(
            P("wide", "tp", None, None),
            P("wide", "tp", None, None),
            P(None, "wide", "tp", None),
        ),
        check_vma=False,
    )
```

```python
import functools
import math

import jax
import jax.numpy as jnp
from jax import lax
from jax.experimental import pallas as pl
from jax.experimental.pallas import tpu as pltpu
from jax.sharding import PartitionSpec as P

NT = (((1,), (1,)), ((), ()))
NN = (((1,), (0,)), ((), ()))
TN = (((0,), (0,)), ((), ()))
OUT_OF_REACH = -2e38
DOCUMENT_STACK = 8
QUERY_STACK = 4
VMEM_BYTES = 48 * 1024 * 1024


def dot(a, b, dims):
    return lax.dot_general(a, b, dims, preferred_element_type=jnp.float32)


def documents(ids_ref, subs, sub):
    uses, rollouts = ids_ref.shape
    place = lax.broadcasted_iota(jnp.int32, (uses, rollouts), 1)
    mine = place == lax.axis_index("wide") * subs + sub
    ids = jnp.where(mine, ids_ref[...].astype(jnp.float32), 0.0)
    return jnp.sum(ids, axis=1, keepdims=True).astype(jnp.int32)


def length_row(subs, kv_heads, slots, ids_ref, lengths_ref):
    mine = documents(ids_ref, subs, lax.axis_index("tp") // kv_heads)
    uses, docs = ids_ref.shape[0], lengths_ref.shape[1]
    column = lax.broadcasted_iota(jnp.int32, (uses, docs), 1)
    lengths = jnp.where(mine == column, lengths_ref[...].astype(jnp.float32), 0.0)
    lengths = jnp.sum(lengths, axis=1, keepdims=True)
    use = lax.broadcasted_iota(jnp.int32, (uses, 128), 0)
    lane = lax.broadcasted_iota(jnp.int32, (uses, 128), 1)
    row = jnp.sum(jnp.where(lane % uses == use, lengths, 0.0), axis=0, keepdims=True)
    return jnp.concatenate([row.astype(jnp.int32)] * (slots // 128), axis=1)


class Rollout:
    def __init__(self, stack, uses, q_ref, g_ref, own_ref, doc_ref, limits):
        self.stack = stack
        self.q_ref, self.g_ref = q_ref, g_ref
        sources, _, per_source, self.head_dim = doc_ref.shape
        self.rows = q_ref.shape[0]
        self.heads = q_ref.shape[1] // self.head_dim
        slots = sources * per_source
        self.scale = 1.0 / math.sqrt(self.head_dim)
        self.doc_k = doc_ref[:, 0].reshape(slots, self.head_dim)
        self.doc_v = doc_ref[:, 1].reshape(slots, self.head_dim)
        self.own_k, self.own_v = own_ref[0], own_ref[1]
        token = lax.broadcasted_iota(jnp.int32, (1, slots), 1) // uses
        self.doc_allowed = token < limits
        square = (self.rows, self.rows)
        causal = lax.broadcasted_iota(jnp.int32, square, 1) <= lax.broadcasted_iota(
            jnp.int32, square, 0
        )
        self.causal = jnp.concatenate([causal.astype(jnp.int32)] * stack, axis=0) > 0

    def stacked(self, ref, first):
        return jnp.concatenate(
            [
                ref[:, pl.ds((first + h) * self.head_dim, self.head_dim)]
                for h in range(self.stack)
            ],
            axis=0,
        )

    def unstack(self, ref, first, value):
        for h in range(self.stack):
            ref[:, pl.ds((first + h) * self.head_dim, self.head_dim)] = value[
                h * self.rows : (h + 1) * self.rows
            ]

    def heads_from(self, first):
        low = jnp.bfloat16
        exponent = self.scale * math.log2(math.e)
        q, g = self.stacked(self.q_ref, first), self.stacked(self.g_ref, first)
        s_doc = jnp.where(self.doc_allowed, dot(q, self.doc_k, NT), OUT_OF_REACH)
        s_own = jnp.where(self.causal, dot(q, self.own_k, NT), OUT_OF_REACH)
        top = jnp.maximum(
            jnp.max(s_doc, axis=1, keepdims=True), jnp.max(s_own, axis=1, keepdims=True)
        )
        e_doc = jnp.exp2((s_doc - top) * exponent)
        e_own = jnp.exp2((s_own - top) * exponent)
        total = jnp.sum(e_doc, axis=1, keepdims=True) + jnp.sum(e_own, axis=1, keepdims=True)
        inverse = 1.0 / total
        w_doc, w_own = e_doc * inverse, e_own * inverse
        w_doc_low, w_own_low = w_doc.astype(low), w_own.astype(low)
        att = (dot(w_doc_low, self.doc_v, NN) + dot(w_own_low, self.own_v, NN)).astype(low)
        row_dot = jnp.sum(
            g.astype(jnp.float32) * att.astype(jnp.float32), axis=1, keepdims=True
        )
        ds_doc = (w_doc * (dot(g, self.doc_v, NT) - row_dot)).astype(low)

        def ds_own():
            return (w_own * (dot(g, self.own_v, NT) - row_dot)).astype(low)

        return q, g, w_doc_low, att, ds_doc, ds_own


def limit_kernel(subs, kv_heads, ids_ref, lengths_ref, limit_ref):
    limit_ref[...] = length_row(subs, kv_heads, limit_ref.shape[1], ids_ref, lengths_ref)


def document_kernel(
    uses, q_ref, g_ref, own_ref, limit_ref, doc_ref, dkv_ref, ready_ref, dk_sum, dv_sum
):
    low = jnp.bfloat16
    sources, _, per_source, head_dim = doc_ref.shape
    ready_ref[...] = limit_ref[...]
    rollout = Rollout(DOCUMENT_STACK, uses, q_ref, g_ref, own_ref, doc_ref, limit_ref[...])
    for first in range(0, rollout.heads, rollout.stack):
        q, g, w_doc, _, ds_doc, _ = rollout.heads_from(first)
        dk, dv = dot(q.T, ds_doc, NN), dot(g.T, w_doc, NN)
        if first:
            dk, dv = dk_sum[...] + dk, dv_sum[...] + dv
        if first + rollout.stack < rollout.heads:
            dk_sum[...] = dk
            dv_sum[...] = dv
        else:
            dk = dk.T * rollout.scale
            dkv_ref[:, 0] = dk.astype(low).reshape(sources, per_source, head_dim)
            dkv_ref[:, 1] = dv.T.astype(low).reshape(sources, per_source, head_dim)


def query_kernel(uses, q_ref, g_ref, own_ref, limit_ref, doc_ref, att_ref, dq_ref, ready_ref):
    ready_ref[...] = limit_ref[...]
    rollout = Rollout(QUERY_STACK, uses, q_ref, g_ref, own_ref, doc_ref, limit_ref[...])
    for first in range(0, rollout.heads, rollout.stack):
        _, _, _, att, ds_doc, ds_own = rollout.heads_from(first)
        dq = dot(ds_doc, rollout.doc_k, NN) + dot(ds_own(), rollout.own_k, NN)
        rollout.unstack(att_ref, first, att)
        rollout.unstack(dq_ref, first, (dq * rollout.scale).astype(jnp.bfloat16))


def attention(q, g, own, ids, lengths, docs, subs, kv_heads):
    rows, width = q.shape
    head_dim = own.shape[2]
    slots = docs.size // (2 * head_dim)
    uses = ids.shape[0]
    vmem = pl.BlockSpec(memory_space=pltpu.VMEM)
    pairs = width // head_dim * rows * (slots + rows)

    def call(kernel, out, *args, scratch=()):
        return pl.pallas_call(
            kernel,
            out_shape=out,
            in_specs=[vmem] * len(args),
            out_specs=(vmem,) * len(out),
            scratch_shapes=list(scratch),
            compiler_params=pltpu.CompilerParams(vmem_limit_bytes=VMEM_BYTES),
            cost_estimate=pl.CostEstimate(
                flops=10 * pairs * head_dim,
                bytes_accessed=2 * (2 * q.size + 2 * docs.size),
                transcendentals=pairs,
            ),
        )(*args)

    row = jax.ShapeDtypeStruct((1, slots), jnp.int32)
    limits = local(functools.partial(limit_kernel, subs, kv_heads), row, ids, lengths)
    d_docs, limits = call(
        functools.partial(document_kernel, uses),
        (jax.ShapeDtypeStruct(docs.shape, jnp.bfloat16), row),
        q, g, own, limits, docs,
        scratch=[pltpu.VMEM((head_dim, slots), jnp.float32)] * 2,
    )
    attended, d_query, ready = call(
        functools.partial(query_kernel, uses),
        (jax.ShapeDtypeStruct(q.shape, jnp.bfloat16),) * 2 + (row,),
        q, g, own, limits, docs,
    )
    return attended, d_query, ready, d_docs


def row_of(kind, doc, token, head, docs_here, block_len):
    return ((head * 2 + kind) * docs_here + doc) * block_len + token


def slab_kernel(doc_ref, out_ref):
    copies, per_owner, head_dim = out_ref.shape
    lines = doc_ref[...].reshape(-1, doc_ref.shape[3])
    heads = lines.shape[1] // head_dim
    slab = jnp.concatenate(
        [lines[:, h * head_dim : (h + 1) * head_dim] for h in range(heads)], axis=0
    )
    for i in range(copies):
        out_ref[i] = slab


def total_kernel(parts_ref, out_ref):
    owners, per_owner, head_dim = parts_ref.shape
    total = parts_ref[0].astype(jnp.float32)
    for i in range(1, owners):
        total = total + parts_ref[i].astype(jnp.float32)
    heads = out_ref.shape[3] // head_dim
    lines = per_owner // heads
    whole = jnp.concatenate(
        [total[h * lines : (h + 1) * lines] for h in range(heads)], axis=1
    )
    out_ref[...] = whole.reshape(out_ref.shape)


def select_kernel(ids_ref, every_ref, out_ref, reads_ref, ids_out_ref, rows_ref):
    ids_out_ref[...] = ids_ref[...]
    owners, per_owner, head_dim = every_ref.shape
    subs, kv_heads, _, per_piece, _ = out_ref.shape
    uses = ids_ref.shape[0]
    docs = reads_ref.shape[1]
    docs_here = docs // owners
    block_len = per_piece // uses
    column = lax.broadcasted_iota(jnp.int32, (uses, docs), 1)
    named = column % owners * docs_here + column // owners
    reads = jnp.concatenate(
        [
            (documents(ids_ref, subs, sub) == named).astype(jnp.float32)
            for sub in range(subs)
        ],
        axis=0,
    ).astype(jnp.bfloat16)
    reads_ref[...] = reads
    rows_ref[...] = every_ref[...].astype(jnp.float32).reshape(owners * per_owner, head_dim)
    for kind in range(2):
        found = []
        for token in range(block_len):
            columns = []
            for h in range(kv_heads):
                of_head = [
                    rows_ref[pl.ds(row_of(kind, doc, token, h, docs_here, block_len), owners, stride=per_owner), :]
                    for doc in range(docs_here)
                ]
                columns.append(jnp.concatenate(of_head, axis=0))
            table = jnp.concatenate(columns, axis=1).astype(jnp.bfloat16)
            found.append(dot(reads, table, NN))
        for h in range(kv_heads):
            piece = [
                part[:, h * head_dim : (h + 1) * head_dim].reshape(subs, uses, head_dim)
                for part in found
            ]
            out_ref[:, h, kind] = jnp.concatenate(piece, axis=1).astype(jnp.bfloat16)


def combine_kernel(ready_ref, reads_ref, back_ref, out_ref, rows_ref):
    owners, per_owner, head_dim = out_ref.shape
    subs, kv_heads, _, per_piece, _ = back_ref.shape
    docs_here = reads_ref.shape[1] // owners
    uses = reads_ref.shape[0] // subs
    block_len = per_piece // uses
    reads = reads_ref[...]
    for kind in range(2):
        pieces = [back_ref[:, h, kind].astype(jnp.float32) for h in range(kv_heads)]
        for token in range(block_len):
            table = jnp.concatenate(
                [
                    piece[:, token * uses : (token + 1) * uses].reshape(subs * uses, head_dim)
                    for piece in pieces
                ],
                axis=1,
            ).astype(jnp.bfloat16)
            sums = dot(reads, table, TN)
            for h in range(kv_heads):
                for doc in range(docs_here):
                    row = row_of(kind, doc, token, h, docs_here, block_len)
                    rows_ref[pl.ds(row, owners, stride=per_owner), :] = sums[
                        doc * owners : (doc + 1) * owners, h * head_dim : (h + 1) * head_dim
                    ]
    out_ref[...] = rows_ref[...].astype(jnp.bfloat16).reshape(out_ref.shape)


def local(kernel, out, *args, scratch=(), flops=0):
    vmem = pl.BlockSpec(memory_space=pltpu.VMEM)
    many = isinstance(out, tuple)
    size = sum(x.size * x.dtype.itemsize for x in args)
    return pl.pallas_call(
        kernel,
        out_shape=out,
        in_specs=[vmem] * len(args),
        out_specs=(vmem,) * len(out) if many else vmem,
        scratch_shapes=list(scratch),
        compiler_params=pltpu.CompilerParams(vmem_limit_bytes=16 * 1024 * 1024),
        cost_estimate=pl.CostEstimate(flops=flops, bytes_accessed=2 * size, transcendentals=0),
    )(*args)


def shards(queries, own_kv, doc_kv, doc_lengths, doc_ids, d_out):
    tp_width = lax.axis_size("tp")
    wide_width = lax.axis_size("wide")
    head_dim = own_kv.shape[4]
    kv_heads = doc_kv.shape[3] // head_dim
    subs = tp_width // kv_heads
    docs_here, block_len = doc_kv.shape[1:3]
    uses = doc_ids.shape[1]
    low = jnp.bfloat16
    per_owner = 2 * docs_here * block_len * kv_heads
    per_piece = block_len * uses

    slabs = jax.ShapeDtypeStruct((wide_width, per_owner, head_dim), low)
    pieces = jax.ShapeDtypeStruct((subs, kv_heads, 2, per_piece, head_dim), low)
    reads = jax.ShapeDtypeStruct((subs * uses, wide_width * docs_here), low)
    ids = doc_ids.T
    rows = pltpu.VMEM((wide_width * per_owner, head_dim), jnp.float32)
    flops = 2 * subs * uses * wide_width * docs_here * per_owner // docs_here * head_dim

    every = lax.all_to_all(local(slab_kernel, slabs, doc_kv), "wide", 0, 0, tiled=True)
    picked, reads, ids = local(
        select_kernel, (pieces, reads, jax.ShapeDtypeStruct(ids.shape, ids.dtype)), ids, every, scratch=(rows,), flops=flops
    )
    docs = lax.all_to_all(
        picked.reshape(tp_width, 2, per_piece, head_dim), "tp", 0, 0, tiled=True
    )

    attended, d_query, ready, d_docs = attention(
        queries[0, 0], d_out[0, 0], own_kv[:, 0, 0], ids, doc_lengths[None], docs, subs, kv_heads
    )

    back = lax.all_to_all(d_docs, "tp", 0, 0, tiled=True).reshape(pieces.shape)
    by_doc = local(combine_kernel, slabs, ready, reads, back, scratch=(rows,), flops=flops)
    parts = lax.all_to_all(by_doc, "wide", 0, 0, tiled=True)
    d_doc = local(total_kernel, jax.ShapeDtypeStruct(doc_kv.shape, jnp.float32), parts)
    return attended[None, None], d_query[None, None], d_doc


def solution(mesh):
    placed = (
        P("wide", "tp", None, None),
        P(None, "wide", "tp", None, None),
        P(None, "wide", "tp", None),
        P(),
        P(),
        P("wide", "tp", None, None),
    )
    return jax.shard_map(
        shards,
        mesh=mesh,
        in_specs=placed,
        out_specs=(
            P("wide", "tp", None, None),
            P("wide", "tp", None, None),
            P(None, "wide", "tp", None),
        ),
        check_vma=False,
    )
```

```python
import functools
import math

import jax
import jax.numpy as jnp
from jax import lax
from jax.experimental import pallas as pl
from jax.experimental.pallas import tpu as pltpu
from jax.sharding import PartitionSpec as P

NT = (((1,), (1,)), ((), ()))
NN = (((1,), (0,)), ((), ()))
TN = (((0,), (0,)), ((), ()))
OUT_OF_REACH = -2e38
DOCUMENT_STACK = 8
QUERY_STACK = 4
VMEM_BYTES = 48 * 1024 * 1024


def dot(a, b, dims):
    return lax.dot_general(a, b, dims, preferred_element_type=jnp.float32)


def documents(ids_ref, subs, sub):
    uses, rollouts = ids_ref.shape
    place = lax.broadcasted_iota(jnp.int32, (uses, rollouts), 1)
    mine = place == lax.axis_index("wide") * subs + sub
    ids = jnp.where(mine, ids_ref[...].astype(jnp.float32), 0.0)
    return jnp.sum(ids, axis=1, keepdims=True).astype(jnp.int32)


def length_row(subs, kv_heads, slots, ids_ref, lengths_ref):
    mine = documents(ids_ref, subs, lax.axis_index("tp") // kv_heads)
    uses, docs = ids_ref.shape[0], lengths_ref.shape[1]
    column = lax.broadcasted_iota(jnp.int32, (uses, docs), 1)
    lengths = jnp.where(mine == column, lengths_ref[...].astype(jnp.float32), 0.0)
    lengths = jnp.sum(lengths, axis=1, keepdims=True)
    use = lax.broadcasted_iota(jnp.int32, (uses, 128), 0)
    lane = lax.broadcasted_iota(jnp.int32, (uses, 128), 1)
    row = jnp.sum(jnp.where(lane % uses == use, lengths, 0.0), axis=0, keepdims=True)
    return jnp.concatenate([row.astype(jnp.int32)] * (slots // 128), axis=1)


class Rollout:
    def __init__(self, stack, uses, q_ref, g_ref, own_ref, doc_ref, limits):
        self.stack = stack
        self.q_ref, self.g_ref = q_ref, g_ref
        sources, _, per_source, self.head_dim = doc_ref.shape
        self.rows = q_ref.shape[0]
        self.heads = q_ref.shape[1] // self.head_dim
        slots = sources * per_source
        self.scale = 1.0 / math.sqrt(self.head_dim)
        self.doc_k = doc_ref[:, 0].reshape(slots, self.head_dim)
        self.doc_v = doc_ref[:, 1].reshape(slots, self.head_dim)
        self.own_k, self.own_v = own_ref[0], own_ref[1]
        token = lax.broadcasted_iota(jnp.int32, (1, slots), 1) // uses
        self.doc_allowed = token < limits
        square = (self.rows, self.rows)
        causal = lax.broadcasted_iota(jnp.int32, square, 1) <= lax.broadcasted_iota(
            jnp.int32, square, 0
        )
        self.causal = jnp.concatenate([causal.astype(jnp.int32)] * stack, axis=0) > 0

    def stacked(self, ref, first):
        return jnp.concatenate(
            [
                ref[:, pl.ds((first + h) * self.head_dim, self.head_dim)]
                for h in range(self.stack)
            ],
            axis=0,
        )

    def unstack(self, ref, first, value):
        for h in range(self.stack):
            ref[:, pl.ds((first + h) * self.head_dim, self.head_dim)] = value[
                h * self.rows : (h + 1) * self.rows
            ]

    def heads_from(self, first):
        low = jnp.bfloat16
        exponent = self.scale * math.log2(math.e)
        q, g = self.stacked(self.q_ref, first), self.stacked(self.g_ref, first)
        s_doc = jnp.where(self.doc_allowed, dot(q, self.doc_k, NT), OUT_OF_REACH)
        s_own = jnp.where(self.causal, dot(q, self.own_k, NT), OUT_OF_REACH)
        top = jnp.maximum(
            jnp.max(s_doc, axis=1, keepdims=True), jnp.max(s_own, axis=1, keepdims=True)
        )
        e_doc = jnp.exp2((s_doc - top) * exponent)
        e_own = jnp.exp2((s_own - top) * exponent)
        total = jnp.sum(e_doc, axis=1, keepdims=True) + jnp.sum(e_own, axis=1, keepdims=True)
        inverse = 1.0 / total
        w_doc, w_own = e_doc * inverse, e_own * inverse
        w_doc_low, w_own_low = w_doc.astype(low), w_own.astype(low)
        att = (dot(w_doc_low, self.doc_v, NN) + dot(w_own_low, self.own_v, NN)).astype(low)
        row_dot = jnp.sum(
            g.astype(jnp.float32) * att.astype(jnp.float32), axis=1, keepdims=True
        )
        ds_doc = (w_doc * (dot(g, self.doc_v, NT) - row_dot)).astype(low)

        def ds_own():
            return (w_own * (dot(g, self.own_v, NT) - row_dot)).astype(low)

        return q, g, w_doc_low, att, ds_doc, ds_own


def limit_kernel(subs, kv_heads, after_ref, ids_ref, lengths_ref, limit_ref):
    limit_ref[...] = length_row(subs, kv_heads, limit_ref.shape[1], ids_ref, lengths_ref)


def document_kernel(
    uses, q_ref, g_ref, own_ref, limit_ref, doc_ref, dkv_ref, ready_ref, dk_sum, dv_sum
):
    low = jnp.bfloat16
    sources, _, per_source, head_dim = doc_ref.shape
    ready_ref[...] = limit_ref[...]
    rollout = Rollout(DOCUMENT_STACK, uses, q_ref, g_ref, own_ref, doc_ref, limit_ref[...])
    for first in range(0, rollout.heads, rollout.stack):
        q, g, w_doc, _, ds_doc, _ = rollout.heads_from(first)
        dk, dv = dot(q.T, ds_doc, NN), dot(g.T, w_doc, NN)
        if first:
            dk, dv = dk_sum[...] + dk, dv_sum[...] + dv
        if first + rollout.stack < rollout.heads:
            dk_sum[...] = dk
            dv_sum[...] = dv
        else:
            dk = dk.T * rollout.scale
            dkv_ref[:, 0] = dk.astype(low).reshape(sources, per_source, head_dim)
            dkv_ref[:, 1] = dv.T.astype(low).reshape(sources, per_source, head_dim)


def query_kernel(uses, q_ref, g_ref, own_ref, limit_ref, doc_ref, att_ref, dq_ref, ready_ref):
    ready_ref[...] = limit_ref[...]
    rollout = Rollout(QUERY_STACK, uses, q_ref, g_ref, own_ref, doc_ref, limit_ref[...])
    for first in range(0, rollout.heads, rollout.stack):
        _, _, _, att, ds_doc, ds_own = rollout.heads_from(first)
        dq = dot(ds_doc, rollout.doc_k, NN) + dot(ds_own(), rollout.own_k, NN)
        rollout.unstack(att_ref, first, att)
        rollout.unstack(dq_ref, first, (dq * rollout.scale).astype(jnp.bfloat16))


def attention(q, g, own, reads, ids, lengths, docs, subs, kv_heads):
    rows, width = q.shape
    head_dim = own.shape[2]
    slots = docs.size // (2 * head_dim)
    uses = ids.shape[0]
    vmem = pl.BlockSpec(memory_space=pltpu.VMEM)
    pairs = width // head_dim * rows * (slots + rows)

    def call(kernel, out, *args, scratch=()):
        return pl.pallas_call(
            kernel,
            out_shape=out,
            in_specs=[vmem] * len(args),
            out_specs=(vmem,) * len(out),
            scratch_shapes=list(scratch),
            compiler_params=pltpu.CompilerParams(vmem_limit_bytes=VMEM_BYTES),
            cost_estimate=pl.CostEstimate(
                flops=10 * pairs * head_dim,
                bytes_accessed=2 * (2 * q.size + 2 * docs.size),
                transcendentals=pairs,
            ),
        )(*args)

    row = jax.ShapeDtypeStruct((1, slots), jnp.int32)
    limits = local(functools.partial(limit_kernel, subs, kv_heads), row, reads, ids, lengths)
    d_docs, limits = call(
        functools.partial(document_kernel, uses),
        (jax.ShapeDtypeStruct(docs.shape, jnp.bfloat16), row),
        q, g, own, limits, docs,
        scratch=[pltpu.VMEM((head_dim, slots), jnp.float32)] * 2,
    )
    attended, d_query, ready = call(
        functools.partial(query_kernel, uses),
        (jax.ShapeDtypeStruct(q.shape, jnp.bfloat16),) * 2 + (row,),
        q, g, own, limits, docs,
    )
    return attended, d_query, ready, d_docs


def row_of(kind, doc, token, head, docs_here, block_len):
    return ((head * 2 + kind) * docs_here + doc) * block_len + token


def slab_kernel(doc_ref, out_ref):
    copies, per_owner, head_dim = out_ref.shape
    lines = doc_ref[...].reshape(-1, doc_ref.shape[3])
    heads = lines.shape[1] // head_dim
    slab = jnp.concatenate(
        [lines[:, h * head_dim : (h + 1) * head_dim] for h in range(heads)], axis=0
    )
    for i in range(copies):
        out_ref[i] = slab


def total_kernel(parts_ref, out_ref):
    owners, per_owner, head_dim = parts_ref.shape
    total = parts_ref[0].astype(jnp.float32)
    for i in range(1, owners):
        total = total + parts_ref[i].astype(jnp.float32)
    heads = out_ref.shape[3] // head_dim
    lines = per_owner // heads
    whole = jnp.concatenate(
        [total[h * lines : (h + 1) * lines] for h in range(heads)], axis=1
    )
    out_ref[...] = whole.reshape(out_ref.shape)


def select_kernel(ids_ref, every_ref, out_ref, reads_ref, rows_ref):
    owners, per_owner, head_dim = every_ref.shape
    subs, kv_heads, _, per_piece, _ = out_ref.shape
    uses = ids_ref.shape[0]
    docs = reads_ref.shape[1]
    docs_here = docs // owners
    block_len = per_piece // uses
    column = lax.broadcasted_iota(jnp.int32, (uses, docs), 1)
    named = column % owners * docs_here + column // owners
    reads = jnp.concatenate(
        [
            (documents(ids_ref, subs, sub) == named).astype(jnp.float32)
            for sub in range(subs)
        ],
        axis=0,
    ).astype(jnp.bfloat16)
    reads_ref[...] = reads
    rows_ref[...] = every_ref[...].astype(jnp.float32).reshape(owners * per_owner, head_dim)
    for kind in range(2):
        found = []
        for token in range(block_len):
            columns = []
            for h in range(kv_heads):
                of_head = [
                    rows_ref[pl.ds(row_of(kind, doc, token, h, docs_here, block_len), owners, stride=per_owner), :]
                    for doc in range(docs_here)
                ]
                columns.append(jnp.concatenate(of_head, axis=0))
            table = jnp.concatenate(columns, axis=1).astype(jnp.bfloat16)
            found.append(dot(reads, table, NN))
        for h in range(kv_heads):
            piece = [
                part[:, h * head_dim : (h + 1) * head_dim].reshape(subs, uses, head_dim)
                for part in found
            ]
            out_ref[:, h, kind] = jnp.concatenate(piece, axis=1).astype(jnp.bfloat16)


def combine_kernel(ready_ref, reads_ref, back_ref, out_ref, rows_ref):
    owners, per_owner, head_dim = out_ref.shape
    subs, kv_heads, _, per_piece, _ = back_ref.shape
    docs_here = reads_ref.shape[1] // owners
    uses = reads_ref.shape[0] // subs
    block_len = per_piece // uses
    reads = reads_ref[...]
    for kind in range(2):
        pieces = [back_ref[:, h, kind].astype(jnp.float32) for h in range(kv_heads)]
        for token in range(block_len):
            table = jnp.concatenate(
                [
                    piece[:, token * uses : (token + 1) * uses].reshape(subs * uses, head_dim)
                    for piece in pieces
                ],
                axis=1,
            ).astype(jnp.bfloat16)
            sums = dot(reads, table, TN)
            for h in range(kv_heads):
                for doc in range(docs_here):
                    row = row_of(kind, doc, token, h, docs_here, block_len)
                    rows_ref[pl.ds(row, owners, stride=per_owner), :] = sums[
                        doc * owners : (doc + 1) * owners, h * head_dim : (h + 1) * head_dim
                    ]
    out_ref[...] = rows_ref[...].astype(jnp.bfloat16).reshape(out_ref.shape)


def local(kernel, out, *args, scratch=(), flops=0):
    vmem = pl.BlockSpec(memory_space=pltpu.VMEM)
    many = isinstance(out, tuple)
    size = sum(x.size * x.dtype.itemsize for x in args)
    return pl.pallas_call(
        kernel,
        out_shape=out,
        in_specs=[vmem] * len(args),
        out_specs=(vmem,) * len(out) if many else vmem,
        scratch_shapes=list(scratch),
        compiler_params=pltpu.CompilerParams(vmem_limit_bytes=16 * 1024 * 1024),
        cost_estimate=pl.CostEstimate(flops=flops, bytes_accessed=2 * size, transcendentals=0),
    )(*args)


def shards(queries, own_kv, doc_kv, doc_lengths, doc_ids, d_out):
    tp_width = lax.axis_size("tp")
    wide_width = lax.axis_size("wide")
    head_dim = own_kv.shape[4]
    kv_heads = doc_kv.shape[3] // head_dim
    subs = tp_width // kv_heads
    docs_here, block_len = doc_kv.shape[1:3]
    uses = doc_ids.shape[1]
    low = jnp.bfloat16
    per_owner = 2 * docs_here * block_len * kv_heads
    per_piece = block_len * uses

    slabs = jax.ShapeDtypeStruct((wide_width, per_owner, head_dim), low)
    pieces = jax.ShapeDtypeStruct((subs, kv_heads, 2, per_piece, head_dim), low)
    reads = jax.ShapeDtypeStruct((subs * uses, wide_width * docs_here), low)
    ids = doc_ids.T
    rows = pltpu.VMEM((wide_width * per_owner, head_dim), jnp.float32)
    flops = 2 * subs * uses * wide_width * docs_here * per_owner // docs_here * head_dim

    every = lax.all_to_all(local(slab_kernel, slabs, doc_kv), "wide", 0, 0, tiled=True)
    picked, reads = local(
        select_kernel, (pieces, reads), ids, every, scratch=(rows,), flops=flops
    )
    docs = lax.all_to_all(
        picked.reshape(tp_width, 2, per_piece, head_dim), "tp", 0, 0, tiled=True
    )

    attended, d_query, ready, d_docs = attention(
        queries[0, 0], d_out[0, 0], own_kv[:, 0, 0], reads, ids, doc_lengths[None], docs, subs, kv_heads
    )

    back = lax.all_to_all(d_docs, "tp", 0, 0, tiled=True).reshape(pieces.shape)
    by_doc = local(combine_kernel, slabs, ready, reads, back, scratch=(rows,), flops=flops)
    parts = lax.all_to_all(by_doc, "wide", 0, 0, tiled=True)
    d_doc = local(total_kernel, jax.ShapeDtypeStruct(doc_kv.shape, jnp.float32), parts)
    return attended[None, None], d_query[None, None], d_doc


def solution(mesh):
    placed = (
        P("wide", "tp", None, None),
        P(None, "wide", "tp", None, None),
        P(None, "wide", "tp", None),
        P(),
        P(),
        P("wide", "tp", None, None),
    )
    return jax.shard_map(
        shards,
        mesh=mesh,
        in_specs=placed,
        out_specs=(
            P("wide", "tp", None, None),
            P("wide", "tp", None, None),
            P(None, "wide", "tp", None),
        ),
        check_vma=False,
    )
```

```python
import functools
import math

import jax
import jax.numpy as jnp
from jax import lax
from jax.experimental import pallas as pl
from jax.experimental.pallas import tpu as pltpu
from jax.sharding import PartitionSpec as P

NT = (((1,), (1,)), ((), ()))
NN = (((1,), (0,)), ((), ()))
TN = (((0,), (0,)), ((), ()))
OUT_OF_REACH = -2e38
DOCUMENT_STACK = 8
QUERY_STACK = 4
VMEM_BYTES = 48 * 1024 * 1024


def dot(a, b, dims):
    return lax.dot_general(a, b, dims, preferred_element_type=jnp.float32)


def documents(ids_ref, subs, sub):
    uses, rollouts = ids_ref.shape
    place = lax.broadcasted_iota(jnp.int32, (uses, rollouts), 1)
    mine = place == lax.axis_index("wide") * subs + sub
    ids = jnp.where(mine, ids_ref[...].astype(jnp.float32), 0.0)
    return jnp.sum(ids, axis=1, keepdims=True).astype(jnp.int32)


def length_row(subs, kv_heads, slots, ids_ref, lengths_ref):
    mine = documents(ids_ref, subs, lax.axis_index("tp") // kv_heads)
    uses, docs = ids_ref.shape[0], lengths_ref.shape[1]
    column = lax.broadcasted_iota(jnp.int32, (uses, docs), 1)
    lengths = jnp.where(mine == column, lengths_ref[...].astype(jnp.float32), 0.0)
    lengths = jnp.sum(lengths, axis=1, keepdims=True)
    use = lax.broadcasted_iota(jnp.int32, (uses, 128), 0)
    lane = lax.broadcasted_iota(jnp.int32, (uses, 128), 1)
    row = jnp.sum(jnp.where(lane % uses == use, lengths, 0.0), axis=0, keepdims=True)
    return jnp.concatenate([row.astype(jnp.int32)] * (slots // 128), axis=1)


class Rollout:
    def __init__(self, stack, uses, q_ref, g_ref, own_ref, doc_ref, limits):
        self.stack = stack
        self.q_ref, self.g_ref = q_ref, g_ref
        sources, _, per_source, self.head_dim = doc_ref.shape
        self.rows = q_ref.shape[0]
        self.heads = q_ref.shape[1] // self.head_dim
        slots = sources * per_source
        self.scale = 1.0 / math.sqrt(self.head_dim)
        self.doc_k = doc_ref[:, 0].reshape(slots, self.head_dim)
        self.doc_v = doc_ref[:, 1].reshape(slots, self.head_dim)
        self.own_k, self.own_v = own_ref[0], own_ref[1]
        token = lax.broadcasted_iota(jnp.int32, (1, slots), 1) // uses
        self.doc_allowed = token < limits
        square = (self.rows, self.rows)
        causal = lax.broadcasted_iota(jnp.int32, square, 1) <= lax.broadcasted_iota(
            jnp.int32, square, 0
        )
        self.causal = jnp.concatenate([causal.astype(jnp.int32)] * stack, axis=0) > 0

    def stacked(self, ref, first):
        return jnp.concatenate(
            [
                ref[:, pl.ds((first + h) * self.head_dim, self.head_dim)]
                for h in range(self.stack)
            ],
            axis=0,
        )

    def unstack(self, ref, first, value):
        for h in range(self.stack):
            ref[:, pl.ds((first + h) * self.head_dim, self.head_dim)] = value[
                h * self.rows : (h + 1) * self.rows
            ]

    def heads_from(self, first):
        low = jnp.bfloat16
        exponent = self.scale * math.log2(math.e)
        q, g = self.stacked(self.q_ref, first), self.stacked(self.g_ref, first)
        s_doc = jnp.where(self.doc_allowed, dot(q, self.doc_k, NT), OUT_OF_REACH)
        s_own = jnp.where(self.causal, dot(q, self.own_k, NT), OUT_OF_REACH)
        top = jnp.maximum(
            jnp.max(s_doc, axis=1, keepdims=True), jnp.max(s_own, axis=1, keepdims=True)
        )
        e_doc = jnp.exp2((s_doc - top) * exponent)
        e_own = jnp.exp2((s_own - top) * exponent)
        total = jnp.sum(e_doc, axis=1, keepdims=True) + jnp.sum(e_own, axis=1, keepdims=True)
        inverse = 1.0 / total
        w_doc, w_own = e_doc * inverse, e_own * inverse
        w_doc_low, w_own_low = w_doc.astype(low), w_own.astype(low)
        att = (dot(w_doc_low, self.doc_v, NN) + dot(w_own_low, self.own_v, NN)).astype(low)
        row_dot = jnp.sum(
            g.astype(jnp.float32) * att.astype(jnp.float32), axis=1, keepdims=True
        )
        ds_doc = (w_doc * (dot(g, self.doc_v, NT) - row_dot)).astype(low)

        def ds_own():
            return (w_own * (dot(g, self.own_v, NT) - row_dot)).astype(low)

        return q, g, w_doc_low, att, ds_doc, ds_own


def document_kernel(
    subs, kv_heads, q_ref, g_ref, own_ref, ids_ref, lengths_ref, doc_ref, dkv_ref, limit_ref, dk_sum, dv_sum
):
    low = jnp.bfloat16
    sources, _, per_source, head_dim = doc_ref.shape
    limits = length_row(subs, kv_heads, sources * per_source, ids_ref, lengths_ref)
    limit_ref[...] = limits
    rollout = Rollout(DOCUMENT_STACK, ids_ref.shape[0], q_ref, g_ref, own_ref, doc_ref, limits)
    for first in range(0, rollout.heads, rollout.stack):
        q, g, w_doc, _, ds_doc, _ = rollout.heads_from(first)
        dk, dv = dot(q.T, ds_doc, NN), dot(g.T, w_doc, NN)
        if first:
            dk, dv = dk_sum[...] + dk, dv_sum[...] + dv
        if first + rollout.stack < rollout.heads:
            dk_sum[...] = dk
            dv_sum[...] = dv
        else:
            dk = dk.T * rollout.scale
            dkv_ref[:, 0] = dk.astype(low).reshape(sources, per_source, head_dim)
            dkv_ref[:, 1] = dv.T.astype(low).reshape(sources, per_source, head_dim)


def query_kernel(uses, q_ref, g_ref, own_ref, limit_ref, doc_ref, att_ref, dq_ref, ready_ref):
    ready_ref[...] = limit_ref[...]
    rollout = Rollout(QUERY_STACK, uses, q_ref, g_ref, own_ref, doc_ref, limit_ref[...])
    for first in range(0, rollout.heads, rollout.stack):
        _, _, _, att, ds_doc, ds_own = rollout.heads_from(first)
        dq = dot(ds_doc, rollout.doc_k, NN) + dot(ds_own(), rollout.own_k, NN)
        rollout.unstack(att_ref, first, att)
        rollout.unstack(dq_ref, first, (dq * rollout.scale).astype(jnp.bfloat16))


def attention(q, g, own, ids, lengths, docs, subs, kv_heads):
    rows, width = q.shape
    head_dim = own.shape[2]
    slots = docs.size // (2 * head_dim)
    uses = ids.shape[0]
    vmem = pl.BlockSpec(memory_space=pltpu.VMEM)
    pairs = width // head_dim * rows * (slots + rows)

    def call(kernel, out, *args, scratch=()):
        return pl.pallas_call(
            kernel,
            out_shape=out,
            in_specs=[vmem] * len(args),
            out_specs=(vmem,) * len(out),
            scratch_shapes=list(scratch),
            compiler_params=pltpu.CompilerParams(vmem_limit_bytes=VMEM_BYTES),
            cost_estimate=pl.CostEstimate(
                flops=10 * pairs * head_dim,
                bytes_accessed=2 * (2 * q.size + 2 * docs.size),
                transcendentals=pairs,
            ),
        )(*args)

    d_docs, limits = call(
        functools.partial(document_kernel, subs, kv_heads),
        (
            jax.ShapeDtypeStruct(docs.shape, jnp.bfloat16),
            jax.ShapeDtypeStruct((1, slots), jnp.int32),
        ),
        q, g, own, ids, lengths, docs,
        scratch=[pltpu.VMEM((head_dim, slots), jnp.float32)] * 2,
    )
    attended, d_query, ready = call(
        functools.partial(query_kernel, uses),
        (jax.ShapeDtypeStruct(q.shape, jnp.bfloat16),) * 2
        + (jax.ShapeDtypeStruct(limits.shape, limits.dtype),),
        q, g, own, limits, docs,
    )
    return attended, d_query, ready, d_docs


def row_of(kind, doc, token, head, docs_here, block_len):
    return ((head * 2 + kind) * docs_here + doc) * block_len + token


def slab_kernel(doc_ref, out_ref):
    copies, per_owner, head_dim = out_ref.shape
    lines = doc_ref[...].reshape(-1, doc_ref.shape[3])
    heads = lines.shape[1] // head_dim
    slab = jnp.concatenate(
        [lines[:, h * head_dim : (h + 1) * head_dim] for h in range(heads)], axis=0
    )
    for i in range(copies):
        out_ref[i] = slab


def total_kernel(parts_ref, out_ref):
    owners, per_owner, head_dim = parts_ref.shape
    total = parts_ref[0].astype(jnp.float32)
    for i in range(1, owners):
        total = total + parts_ref[i].astype(jnp.float32)
    heads = out_ref.shape[3] // head_dim
    lines = per_owner // heads
    whole = jnp.concatenate(
        [total[h * lines : (h + 1) * lines] for h in range(heads)], axis=1
    )
    out_ref[...] = whole.reshape(out_ref.shape)


def select_kernel(ids_ref, every_ref, out_ref, reads_ref, rows_ref):
    owners, per_owner, head_dim = every_ref.shape
    subs, kv_heads, _, per_piece, _ = out_ref.shape
    uses = ids_ref.shape[0]
    docs = reads_ref.shape[1]
    docs_here = docs // owners
    block_len = per_piece // uses
    column = lax.broadcasted_iota(jnp.int32, (uses, docs), 1)
    named = column % owners * docs_here + column // owners
    reads = jnp.concatenate(
        [
            (documents(ids_ref, subs, sub) == named).astype(jnp.float32)
            for sub in range(subs)
        ],
        axis=0,
    ).astype(jnp.bfloat16)
    reads_ref[...] = reads
    rows_ref[...] = every_ref[...].astype(jnp.float32).reshape(owners * per_owner, head_dim)
    for kind in range(2):
        found = []
        for token in range(block_len):
            columns = []
            for h in range(kv_heads):
                of_head = [
                    rows_ref[pl.ds(row_of(kind, doc, token, h, docs_here, block_len), owners, stride=per_owner), :]
                    for doc in range(docs_here)
                ]
                columns.append(jnp.concatenate(of_head, axis=0))
            table = jnp.concatenate(columns, axis=1).astype(jnp.bfloat16)
            found.append(dot(reads, table, NN))
        for h in range(kv_heads):
            piece = [
                part[:, h * head_dim : (h + 1) * head_dim].reshape(subs, uses, head_dim)
                for part in found
            ]
            out_ref[:, h, kind] = jnp.concatenate(piece, axis=1).astype(jnp.bfloat16)


def combine_kernel(ready_ref, reads_ref, back_ref, out_ref, rows_ref):
    owners, per_owner, head_dim = out_ref.shape
    subs, kv_heads, _, per_piece, _ = back_ref.shape
    docs_here = reads_ref.shape[1] // owners
    uses = reads_ref.shape[0] // subs
    block_len = per_piece // uses
    reads = reads_ref[...]
    for kind in range(2):
        pieces = [back_ref[:, h, kind].astype(jnp.float32) for h in range(kv_heads)]
        for token in range(block_len):
            table = jnp.concatenate(
                [
                    piece[:, token * uses : (token + 1) * uses].reshape(subs * uses, head_dim)
                    for piece in pieces
                ],
                axis=1,
            ).astype(jnp.bfloat16)
            sums = dot(reads, table, TN)
            for h in range(kv_heads):
                for doc in range(docs_here):
                    row = row_of(kind, doc, token, h, docs_here, block_len)
                    rows_ref[pl.ds(row, owners, stride=per_owner), :] = sums[
                        doc * owners : (doc + 1) * owners, h * head_dim : (h + 1) * head_dim
                    ]
    out_ref[...] = rows_ref[...].astype(jnp.bfloat16).reshape(out_ref.shape)


def local(kernel, out, *args, scratch=(), flops=0):
    vmem = pl.BlockSpec(memory_space=pltpu.VMEM)
    many = isinstance(out, tuple)
    size = sum(x.size * x.dtype.itemsize for x in args)
    return pl.pallas_call(
        kernel,
        out_shape=out,
        in_specs=[vmem] * len(args),
        out_specs=(vmem,) * len(out) if many else vmem,
        scratch_shapes=list(scratch),
        compiler_params=pltpu.CompilerParams(vmem_limit_bytes=16 * 1024 * 1024),
        cost_estimate=pl.CostEstimate(flops=flops, bytes_accessed=2 * size, transcendentals=0),
    )(*args)


def shards(queries, own_kv, doc_kv, doc_lengths, doc_ids, d_out):
    tp_width = lax.axis_size("tp")
    wide_width = lax.axis_size("wide")
    head_dim = own_kv.shape[4]
    kv_heads = doc_kv.shape[3] // head_dim
    subs = tp_width // kv_heads
    docs_here, block_len = doc_kv.shape[1:3]
    uses = doc_ids.shape[1]
    low = jnp.bfloat16
    per_owner = 2 * docs_here * block_len * kv_heads
    per_piece = block_len * uses

    slabs = jax.ShapeDtypeStruct((wide_width, per_owner, head_dim), low)
    pieces = jax.ShapeDtypeStruct((subs, kv_heads, 2, per_piece, head_dim), low)
    reads = jax.ShapeDtypeStruct((subs * uses, wide_width * docs_here), low)
    ids = doc_ids.T
    rows = pltpu.VMEM((wide_width * per_owner, head_dim), jnp.float32)
    flops = 2 * subs * uses * wide_width * docs_here * per_owner // docs_here * head_dim

    every = lax.all_to_all(local(slab_kernel, slabs, doc_kv), "wide", 0, 0, tiled=True)
    picked, reads = local(
        select_kernel, (pieces, reads), ids, every, scratch=(rows,), flops=flops
    )
    docs = lax.all_to_all(
        picked.reshape(tp_width, 2, per_piece, head_dim), "tp", 0, 0, tiled=True
    )

    attended, d_query, ready, d_docs = attention(
        queries[0, 0], d_out[0, 0], own_kv[:, 0, 0], ids, doc_lengths[None], docs, subs, kv_heads
    )

    back = lax.all_to_all(d_docs, "tp", 0, 0, tiled=True).reshape(pieces.shape)
    by_doc = local(combine_kernel, slabs, ready, reads, back, scratch=(rows,), flops=flops)
    parts = lax.all_to_all(by_doc, "wide", 0, 0, tiled=True)
    d_doc = local(total_kernel, jax.ShapeDtypeStruct(doc_kv.shape, jnp.float32), parts)
    return attended[None, None], d_query[None, None], d_doc


def solution(mesh):
    placed = (
        P("wide", "tp", None, None),
        P(None, "wide", "tp", None, None),
        P(None, "wide", "tp", None),
        P(),
        P(),
        P("wide", "tp", None, None),
    )
    return jax.shard_map(
        shards,
        mesh=mesh,
        in_specs=placed,
        out_specs=(
            P("wide", "tp", None, None),
            P("wide", "tp", None, None),
            P(None, "wide", "tp", None),
        ),
        check_vma=False,
    )
```

```python
import functools
import math

import jax
import jax.numpy as jnp
from jax import lax
from jax.experimental import pallas as pl
from jax.experimental.pallas import tpu as pltpu
from jax.sharding import PartitionSpec as P

NT = (((1,), (1,)), ((), ()))
NN = (((1,), (0,)), ((), ()))
TN = (((0,), (0,)), ((), ()))
OUT_OF_REACH = -2e38
DOCUMENT_STACK = 8
QUERY_STACK = 4
VMEM_BYTES = 48 * 1024 * 1024


def dot(a, b, dims):
    return lax.dot_general(a, b, dims, preferred_element_type=jnp.float32)


def documents(ids_ref, subs, sub):
    uses, rollouts = ids_ref.shape
    place = lax.broadcasted_iota(jnp.int32, (uses, rollouts), 1)
    mine = place == lax.axis_index("wide") * subs + sub
    ids = jnp.where(mine, ids_ref[...].astype(jnp.float32), 0.0)
    return jnp.sum(ids, axis=1, keepdims=True).astype(jnp.int32)


def length_row(subs, kv_heads, slots, ids_ref, lengths_ref):
    mine = documents(ids_ref, subs, lax.axis_index("tp") // kv_heads)
    uses, docs = ids_ref.shape[0], lengths_ref.shape[0]
    column = lax.broadcasted_iota(jnp.int32, (uses, docs), 1)
    lengths = jnp.zeros((uses, docs), jnp.int32)
    for doc in range(docs):
        lengths = jnp.where(column == doc, lengths_ref[doc], lengths)
    lengths = jnp.where(mine == column, lengths.astype(jnp.float32), 0.0)
    lengths = jnp.sum(lengths, axis=1, keepdims=True)
    use = lax.broadcasted_iota(jnp.int32, (uses, 128), 0)
    lane = lax.broadcasted_iota(jnp.int32, (uses, 128), 1)
    row = jnp.sum(jnp.where(lane % uses == use, lengths, 0.0), axis=0, keepdims=True)
    return jnp.concatenate([row.astype(jnp.int32)] * (slots // 128), axis=1)


class Rollout:
    def __init__(self, stack, uses, q_ref, g_ref, own_ref, doc_ref, limits):
        self.stack = stack
        self.q_ref, self.g_ref = q_ref, g_ref
        sources, _, per_source, self.head_dim = doc_ref.shape
        self.rows = q_ref.shape[0]
        self.heads = q_ref.shape[1] // self.head_dim
        slots = sources * per_source
        self.scale = 1.0 / math.sqrt(self.head_dim)
        self.doc_k = doc_ref[:, 0].reshape(slots, self.head_dim)
        self.doc_v = doc_ref[:, 1].reshape(slots, self.head_dim)
        self.own_k, self.own_v = own_ref[0], own_ref[1]
        token = lax.broadcasted_iota(jnp.int32, (1, slots), 1) // uses
        self.doc_allowed = token < limits
        square = (self.rows, self.rows)
        causal = lax.broadcasted_iota(jnp.int32, square, 1) <= lax.broadcasted_iota(
            jnp.int32, square, 0
        )
        self.causal = jnp.concatenate([causal.astype(jnp.int32)] * stack, axis=0) > 0

    def stacked(self, ref, first):
        return jnp.concatenate(
            [
                ref[:, pl.ds((first + h) * self.head_dim, self.head_dim)]
                for h in range(self.stack)
            ],
            axis=0,
        )

    def unstack(self, ref, first, value):
        for h in range(self.stack):
            ref[:, pl.ds((first + h) * self.head_dim, self.head_dim)] = value[
                h * self.rows : (h + 1) * self.rows
            ]

    def heads_from(self, first):
        low = jnp.bfloat16
        exponent = self.scale * math.log2(math.e)
        q, g = self.stacked(self.q_ref, first), self.stacked(self.g_ref, first)
        s_doc = jnp.where(self.doc_allowed, dot(q, self.doc_k, NT), OUT_OF_REACH)
        s_own = jnp.where(self.causal, dot(q, self.own_k, NT), OUT_OF_REACH)
        top = jnp.maximum(
            jnp.max(s_doc, axis=1, keepdims=True), jnp.max(s_own, axis=1, keepdims=True)
        )
        e_doc = jnp.exp2((s_doc - top) * exponent)
        e_own = jnp.exp2((s_own - top) * exponent)
        total = jnp.sum(e_doc, axis=1, keepdims=True) + jnp.sum(e_own, axis=1, keepdims=True)
        inverse = 1.0 / total
        w_doc, w_own = e_doc * inverse, e_own * inverse
        w_doc_low, w_own_low = w_doc.astype(low), w_own.astype(low)
        att = (dot(w_doc_low, self.doc_v, NN) + dot(w_own_low, self.own_v, NN)).astype(low)
        row_dot = jnp.sum(
            g.astype(jnp.float32) * att.astype(jnp.float32), axis=1, keepdims=True
        )
        ds_doc = (w_doc * (dot(g, self.doc_v, NT) - row_dot)).astype(low)

        def ds_own():
            return (w_own * (dot(g, self.own_v, NT) - row_dot)).astype(low)

        return q, g, w_doc_low, att, ds_doc, ds_own


def document_kernel(
    subs, kv_heads, q_ref, g_ref, own_ref, ids_ref, lengths_ref, doc_ref, dkv_ref, limit_ref, dk_sum, dv_sum
):
    low = jnp.bfloat16
    sources, _, per_source, head_dim = doc_ref.shape
    limits = length_row(subs, kv_heads, sources * per_source, ids_ref, lengths_ref)
    limit_ref[...] = limits
    rollout = Rollout(DOCUMENT_STACK, ids_ref.shape[0], q_ref, g_ref, own_ref, doc_ref, limits)
    for first in range(0, rollout.heads, rollout.stack):
        q, g, w_doc, _, ds_doc, _ = rollout.heads_from(first)
        dk, dv = dot(q.T, ds_doc, NN), dot(g.T, w_doc, NN)
        if first:
            dk, dv = dk_sum[...] + dk, dv_sum[...] + dv
        if first + rollout.stack < rollout.heads:
            dk_sum[...] = dk
            dv_sum[...] = dv
        else:
            dk = dk.T * rollout.scale
            dkv_ref[:, 0] = dk.astype(low).reshape(sources, per_source, head_dim)
            dkv_ref[:, 1] = dv.T.astype(low).reshape(sources, per_source, head_dim)


def query_kernel(uses, q_ref, g_ref, own_ref, limit_ref, doc_ref, att_ref, dq_ref, ready_ref):
    ready_ref[...] = limit_ref[...]
    rollout = Rollout(QUERY_STACK, uses, q_ref, g_ref, own_ref, doc_ref, limit_ref[...])
    for first in range(0, rollout.heads, rollout.stack):
        _, _, _, att, ds_doc, ds_own = rollout.heads_from(first)
        dq = dot(ds_doc, rollout.doc_k, NN) + dot(ds_own(), rollout.own_k, NN)
        rollout.unstack(att_ref, first, att)
        rollout.unstack(dq_ref, first, (dq * rollout.scale).astype(jnp.bfloat16))


def attention(q, g, own, ids, lengths, docs, subs, kv_heads):
    rows, width = q.shape
    head_dim = own.shape[2]
    slots = docs.size // (2 * head_dim)
    uses = ids.shape[0]
    vmem = pl.BlockSpec(memory_space=pltpu.VMEM)
    smem = pl.BlockSpec(memory_space=pltpu.SMEM)
    pairs = width // head_dim * rows * (slots + rows)

    def call(kernel, out, *args, scratch=()):
        return pl.pallas_call(
            kernel,
            out_shape=out,
            in_specs=[smem if x is lengths else vmem for x in args],
            out_specs=(vmem,) * len(out),
            scratch_shapes=list(scratch),
            compiler_params=pltpu.CompilerParams(vmem_limit_bytes=VMEM_BYTES),
            cost_estimate=pl.CostEstimate(
                flops=10 * pairs * head_dim,
                bytes_accessed=2 * (2 * q.size + 2 * docs.size),
                transcendentals=pairs,
            ),
        )(*args)

    d_docs, limits = call(
        functools.partial(document_kernel, subs, kv_heads),
        (
            jax.ShapeDtypeStruct(docs.shape, jnp.bfloat16),
            jax.ShapeDtypeStruct((1, slots), jnp.int32),
        ),
        q, g, own, ids, lengths, docs,
        scratch=[pltpu.VMEM((head_dim, slots), jnp.float32)] * 2,
    )
    attended, d_query, ready = call(
        functools.partial(query_kernel, uses),
        (jax.ShapeDtypeStruct(q.shape, jnp.bfloat16),) * 2
        + (jax.ShapeDtypeStruct(limits.shape, limits.dtype),),
        q, g, own, limits, docs,
    )
    return attended, d_query, ready, d_docs


def row_of(kind, doc, token, head, docs_here, block_len):
    return ((head * 2 + kind) * docs_here + doc) * block_len + token


def slab_kernel(doc_ref, out_ref):
    copies, per_owner, head_dim = out_ref.shape
    lines = doc_ref[...].reshape(-1, doc_ref.shape[3])
    heads = lines.shape[1] // head_dim
    slab = jnp.concatenate(
        [lines[:, h * head_dim : (h + 1) * head_dim] for h in range(heads)], axis=0
    )
    for i in range(copies):
        out_ref[i] = slab


def total_kernel(parts_ref, out_ref):
    owners, per_owner, head_dim = parts_ref.shape
    total = parts_ref[0].astype(jnp.float32)
    for i in range(1, owners):
        total = total + parts_ref[i].astype(jnp.float32)
    heads = out_ref.shape[3] // head_dim
    lines = per_owner // heads
    whole = jnp.concatenate(
        [total[h * lines : (h + 1) * lines] for h in range(heads)], axis=1
    )
    out_ref[...] = whole.reshape(out_ref.shape)


def select_kernel(ids_ref, every_ref, out_ref, reads_ref, rows_ref):
    owners, per_owner, head_dim = every_ref.shape
    subs, kv_heads, _, per_piece, _ = out_ref.shape
    uses = ids_ref.shape[0]
    docs = reads_ref.shape[1]
    docs_here = docs // owners
    block_len = per_piece // uses
    column = lax.broadcasted_iota(jnp.int32, (uses, docs), 1)
    named = column % owners * docs_here + column // owners
    reads = jnp.concatenate(
        [
            (documents(ids_ref, subs, sub) == named).astype(jnp.float32)
            for sub in range(subs)
        ],
        axis=0,
    ).astype(jnp.bfloat16)
    reads_ref[...] = reads
    rows_ref[...] = every_ref[...].astype(jnp.float32).reshape(owners * per_owner, head_dim)
    for kind in range(2):
        found = []
        for token in range(block_len):
            columns = []
            for h in range(kv_heads):
                of_head = [
                    rows_ref[pl.ds(row_of(kind, doc, token, h, docs_here, block_len), owners, stride=per_owner), :]
                    for doc in range(docs_here)
                ]
                columns.append(jnp.concatenate(of_head, axis=0))
            table = jnp.concatenate(columns, axis=1).astype(jnp.bfloat16)
            found.append(dot(reads, table, NN))
        for h in range(kv_heads):
            piece = [
                part[:, h * head_dim : (h + 1) * head_dim].reshape(subs, uses, head_dim)
                for part in found
            ]
            out_ref[:, h, kind] = jnp.concatenate(piece, axis=1).astype(jnp.bfloat16)


def combine_kernel(ready_ref, reads_ref, back_ref, out_ref, rows_ref):
    owners, per_owner, head_dim = out_ref.shape
    subs, kv_heads, _, per_piece, _ = back_ref.shape
    docs_here = reads_ref.shape[1] // owners
    uses = reads_ref.shape[0] // subs
    block_len = per_piece // uses
    reads = reads_ref[...]
    for kind in range(2):
        pieces = [back_ref[:, h, kind].astype(jnp.float32) for h in range(kv_heads)]
        for token in range(block_len):
            table = jnp.concatenate(
                [
                    piece[:, token * uses : (token + 1) * uses].reshape(subs * uses, head_dim)
                    for piece in pieces
                ],
                axis=1,
            ).astype(jnp.bfloat16)
            sums = dot(reads, table, TN)
            for h in range(kv_heads):
                for doc in range(docs_here):
                    row = row_of(kind, doc, token, h, docs_here, block_len)
                    rows_ref[pl.ds(row, owners, stride=per_owner), :] = sums[
                        doc * owners : (doc + 1) * owners, h * head_dim : (h + 1) * head_dim
                    ]
    out_ref[...] = rows_ref[...].astype(jnp.bfloat16).reshape(out_ref.shape)


def local(kernel, out, *args, scratch=(), flops=0):
    vmem = pl.BlockSpec(memory_space=pltpu.VMEM)
    many = isinstance(out, tuple)
    size = sum(x.size * x.dtype.itemsize for x in args)
    return pl.pallas_call(
        kernel,
        out_shape=out,
        in_specs=[vmem] * len(args),
        out_specs=(vmem,) * len(out) if many else vmem,
        scratch_shapes=list(scratch),
        compiler_params=pltpu.CompilerParams(vmem_limit_bytes=16 * 1024 * 1024),
        cost_estimate=pl.CostEstimate(flops=flops, bytes_accessed=2 * size, transcendentals=0),
    )(*args)


def shards(queries, own_kv, doc_kv, doc_lengths, doc_ids, d_out):
    tp_width = lax.axis_size("tp")
    wide_width = lax.axis_size("wide")
    head_dim = own_kv.shape[4]
    kv_heads = doc_kv.shape[3] // head_dim
    subs = tp_width // kv_heads
    docs_here, block_len = doc_kv.shape[1:3]
    uses = doc_ids.shape[1]
    low = jnp.bfloat16
    per_owner = 2 * docs_here * block_len * kv_heads
    per_piece = block_len * uses

    slabs = jax.ShapeDtypeStruct((wide_width, per_owner, head_dim), low)
    pieces = jax.ShapeDtypeStruct((subs, kv_heads, 2, per_piece, head_dim), low)
    reads = jax.ShapeDtypeStruct((subs * uses, wide_width * docs_here), low)
    ids = doc_ids.T
    rows = pltpu.VMEM((wide_width * per_owner, head_dim), jnp.float32)
    flops = 2 * subs * uses * wide_width * docs_here * per_owner // docs_here * head_dim

    every = lax.all_to_all(local(slab_kernel, slabs, doc_kv), "wide", 0, 0, tiled=True)
    picked, reads = local(
        select_kernel, (pieces, reads), ids, every, scratch=(rows,), flops=flops
    )
    docs = lax.all_to_all(
        picked.reshape(tp_width, 2, per_piece, head_dim), "tp", 0, 0, tiled=True
    )

    attended, d_query, ready, d_docs = attention(
        queries[0, 0], d_out[0, 0], own_kv[:, 0, 0], ids, doc_lengths, docs, subs, kv_heads
    )

    back = lax.all_to_all(d_docs, "tp", 0, 0, tiled=True).reshape(pieces.shape)
    by_doc = local(combine_kernel, slabs, ready, reads, back, scratch=(rows,), flops=flops)
    parts = lax.all_to_all(by_doc, "wide", 0, 0, tiled=True)
    d_doc = local(total_kernel, jax.ShapeDtypeStruct(doc_kv.shape, jnp.float32), parts)
    return attended[None, None], d_query[None, None], d_doc


def solution(mesh):
    placed = (
        P("wide", "tp", None, None),
        P(None, "wide", "tp", None, None),
        P(None, "wide", "tp", None),
        P(),
        P(),
        P("wide", "tp", None, None),
    )
    return jax.shard_map(
        shards,
        mesh=mesh,
        in_specs=placed,
        out_specs=(
            P("wide", "tp", None, None),
            P("wide", "tp", None, None),
            P(None, "wide", "tp", None),
        ),
        check_vma=False,
    )
```
